512 devices in a mesh: trip: 64 (over z, x), aux: 8 (over y, core).
Axes of the slice: x: 4, y: 4, z: 16, core: 2. Of those that a mesh axis runs over, the one named last changes fastest.
Arguments:
- aux_blocks: bfloat16 [576, 1024, 1600], P('trip', 'aux'), may hold values from -6 to 6
- occ_blocks: bfloat16 [576, 1024, 120], P('trip', 'aux'), may hold values from -0.03125 to 0.03125
- intersections: bfloat16 [576, 3, 64, 40], P('trip'), may hold values from -0.75 to 0.75
- tno_energy: float32 [576, 40], P('trip'), may hold values from 0.5 to 3
- occ_energy: float32 [576, 3], P('trip'), may hold values from -1 to -0.3
- tno_rank: int32 [576], P('trip'), may hold values from 20 to 40
- triples_old: float32 [576, 40, 1600], P('trip', 'aux'), may hold values from -6 to 6
- pair_amps: bfloat16 [1024, 4096], P('trip'), may hold values from -6 to 6
- pno_energy: float32 [1024, 64], P('trip'), may hold values from 0.5 to 3
- pair_occ: float32 [1024], P('trip'), may hold values from 0.6 to 2
- pair_rank: int32 [1024], P('trip'), may hold values from 16 to 64
- request_owner: int32 [576, 3, 1], P('trip'), may hold values from 0 to 63; in each aligned block of 27 rows (0 to 26, 27 to 53, ..., all dimensions but the last counted through in order) no two rows name the same one
- request_row: int32 [576, 3], P('trip'), may hold values from 0 to 15
Outputs:
- triples_new: float32 [576, 40, 1600], P('trip', 'aux')
- pairs_new: float32 [1024, 4096], P('trip')
The draws below stay inside these ranges and needn't reach their ends.
Inputs may be any that keep to these rules, and one draw needn't show every extreme that they name: `request_owner`: within the rows of one device (aligned blocks of 27 rows), no owner is named by more than 1 row, a bound that some block reaches.
All inputs are finite; a program needn't handle non-finite values.
Results may differ from the reference program's by a relative error of at most 0.022.
Values may be sent and summed in bfloat16 or wider, within the bound.
No kernel may reach another device: no remote copies, remote signals or barrier semaphores. Data moves between devices by JAX's collectives and lax.ppermute only.
A program may use at most 128 MiB of HBM per device.

```python
import math
import jax
import jax.numpy as jnp
import numpy as np
from jax import lax

NT = 40
NPNO = 64
AUXDOM = 1024
PAIRS_DEV = 16
TRIP_DEV = 9
CAP = 1
PASSES = 2
TRIPLES = 576
PAIRS = 1024
N_TRIP = 64
N_AUX = 8


def set_ends(values, rng, low, largest):
    longest = values.shape.index(max(values.shape))
    spots = []
    for shift in (0, 1):
        where = [jax.random.randint(jax.random.fold_in(rng, axis), (), 0, length) for axis, length in enumerate(values.shape)]
        where[longest] = (where[longest] + shift) % values.shape[longest]
        spots.append(tuple(where))
    return values.at[spots[0]].set(low).at[spots[1]].set(largest)


def level_of(rng, shape, cuts, low, high):
    def one(position, parts):
        steps = jax.random.uniform(jax.random.fold_in(jax.random.fold_in(rng, 6), position), (parts,), jnp.float32, low / len(cuts), high / len(cuts))
        return jnp.repeat(jnp.exp(steps), shape[position] // parts).reshape((-1,) + (1,) * (len(shape) - position - 1))

    factor_of = one(*cuts[0])
    for cut in cuts[1:]:
        factor_of = factor_of * one(*cut)
    return factor_of


def assign_block(stream_key, own, number, rows, count, top, bound, lean):
    order = jax.random.permutation(stream_key, count)
    heavy_load, common = portions_of(count, rows * top, bound, lean, True), portions_of(count, rows * top, bound, lean, False)
    places = jnp.arange(count)

    def named(lengths, offset_by):
        used = int((lengths > 0).sum())
        fixed = max(1, used // 4)
        shifted = fixed + (places - fixed + offset_by * (used - fixed)) % max(1, count - fixed)
        return jnp.zeros((count,), jnp.int32).at[order[jnp.where(places < fixed, places, shifted)]].set(jnp.asarray(lengths, jnp.int32))

    lengths = jnp.where(number % 4 == 0, named(heavy_load, number // 4), named(common, number - number // 4 - 1))
    mixed = jax.random.permutation(jax.random.fold_in(own, 3), count)
    giver, sink = mixed[0:count // 2 * 2:2], mixed[1:count // 2 * 2:2]
    room = jnp.minimum(lengths[giver] - 1, bound - lengths[sink]) // 2
    room = jnp.where((giver == order[0]) | (sink == order[0]) | (lengths[sink] == 0), 0, jnp.maximum(room, 0))
    shifted = jax.random.randint(jax.random.fold_in(own, 4), (count // 2,), 0, 1 << 20) % (room + 1)
    lengths = lengths.at[giver].add(-shifted).at[sink].add(shifted)
    members = jnp.searchsorted(jnp.cumsum(lengths), jnp.arange(rows * top), side="right").astype(jnp.int32)
    table = members.reshape(top, rows).T
    table = table[jax.random.permutation(jax.random.fold_in(own, 1), rows)]
    offset_by = jax.random.randint(jax.random.fold_in(own, 2), (rows, 1), 0, top)
    return jnp.take_along_axis(table, (jnp.arange(top)[None, :] + offset_by) % top, axis=1)


def portions_of(count, total, limit, slope, full):
    weights = [(1 << 20) // math.isqrt(grade ** slope) + 1 for grade in range(1, count + 1)]
    largest = limit if full else min(limit, max(-(-total // count), total * weights[0] // sum(weights)))
    least = 1 if total - largest >= count - 1 else 0
    given, rest = [largest] + [least] * (count - 1), total - largest - least * (count - 1)
    while rest > 0:
        free = [i for i in range(1, count) if given[i] < largest] or [i for i in range(1, count) if given[i] < limit]
        mass, budget = sum([weights[i] for i in free]), rest
        for i in free:
            more = min(limit - given[i], max(1, budget * weights[i] // mass), rest)
            given[i] = given[i] + more
            rest = rest - more
    return np.array(given)


def scatter_about(stream_key, shape, scale, limit, cuts=(), kind=jnp.bfloat16):
    gain = level_of(stream_key, shape, cuts, -0.22, 0.18) if cuts else 1.0
    result = jax.random.normal(stream_key, shape, jnp.float32) * scale * gain
    return jnp.minimum(jnp.maximum(result, -limit), limit).astype(kind)


def setup_inputs(seed: int = 0) -> dict:
    streams_of = jax.random.split(jax.random.key(seed), 14)
    aux_blocks = scatter_about(streams_of[0], (TRIPLES, AUXDOM, NT * NT), 1.0, 6.0, ((0, 64), (1, 8)))
    occ_blocks = scatter_about(streams_of[1], (TRIPLES, AUXDOM, 3 * NT), (AUXDOM * NT) ** -0.5, 0.03125, ((0, 64), (1, 8)))
    intersections = scatter_about(streams_of[2], (TRIPLES, 3, NPNO, NT), NPNO ** -0.5, 0.75, ((0, 64),))
    tno_energy = jnp.clip(0.5 + 2.5 * jax.random.uniform(streams_of[3], (TRIPLES, NT), jnp.float32) ** level_of(streams_of[3], (TRIPLES, NT), ((0, 64),), -0.2, 0.2), 0.5, 3.0)
    occ_energy = jnp.clip(-1.0 + 0.7 * jax.random.uniform(streams_of[4], (TRIPLES, 3), jnp.float32) ** level_of(streams_of[4], (TRIPLES, 3), ((0, 64),), -0.2, 0.2), -1.0, -0.3)
    tno_rank = set_ends(jax.random.randint(streams_of[5], (TRIPLES,), NT // 2, NT + 1), jax.random.fold_in(streams_of[5], 1), NT // 2, NT).astype(jnp.int32)
    triples_old = scatter_about(streams_of[6], (TRIPLES, NT, NT * NT), 1.0, 6.0, ((0, 64), (1, 8)), jnp.float32)
    pair_amps = scatter_about(streams_of[7], (PAIRS, NPNO * NPNO), 1.0, 6.0, ((0, 64),))
    pno_energy = jnp.clip(0.5 + 2.5 * jax.random.uniform(streams_of[8], (PAIRS, NPNO), jnp.float32) ** level_of(streams_of[8], (PAIRS, NPNO), ((0, 64),), -0.2, 0.2), 0.5, 3.0)
    pair_occ = jnp.clip(0.6 + 1.4 * jax.random.uniform(streams_of[9], (PAIRS,), jnp.float32) ** level_of(streams_of[9], (PAIRS,), ((0, 64),), -0.2, 0.2), 0.6, 2.0)
    pair_rank = set_ends(jax.random.randint(streams_of[10], (PAIRS,), NPNO // 4, NPNO + 1), jax.random.fold_in(streams_of[10], 1), NPNO // 4, NPNO).astype(jnp.int32)
    request_owner_keys = jax.random.split(jax.random.fold_in(streams_of[11], 1), TRIPLES * 3 // (3 * TRIP_DEV))
    request_owner_turns = jax.random.permutation(jax.random.fold_in(streams_of[11], 3), TRIPLES * 3 // (3 * TRIP_DEV))
    request_owner = jax.vmap(lambda own, number: assign_block(jax.random.fold_in(streams_of[11], 2), own, number, 3 * TRIP_DEV, N_TRIP, 1, CAP, 2))(request_owner_keys, request_owner_turns).reshape((TRIPLES, 3, 1))
    request_row = set_ends(jax.random.randint(streams_of[12], (TRIPLES, 3), 0, PAIRS_DEV), jax.random.fold_in(streams_of[12], 1), 0, PAIRS_DEV - 1).astype(jnp.int32)
    return dict(aux_blocks=aux_blocks, occ_blocks=occ_blocks, intersections=intersections, tno_energy=tno_energy, occ_energy=occ_energy, tno_rank=tno_rank, triples_old=triples_old, pair_amps=pair_amps, pno_energy=pno_energy, pair_occ=pair_occ, pair_rank=pair_rank, request_owner=request_owner, request_row=request_row)


SHIFT_LEVEL = 1.0


def rounded(value):
    return lax.optimization_barrier(value.astype(jnp.bfloat16)).astype(jnp.float32)


def one_triple(inputs):
    xblock, yblock, cover, energy, occupied, rank, amplitude, fetched = inputs
    group = AUXDOM // N_AUX
    xgroups = xblock.reshape(N_AUX, group, NT * NT).astype(jnp.float32)
    ygroups = yblock.reshape(N_AUX, group, 3 * NT).astype(jnp.float32)
    integrals = rounded(jnp.einsum('gqx,gqy->gxy', xgroups, ygroups)).reshape(N_AUX, NT, NT, 3, NT)
    coverf = cover.astype(jnp.float32)
    pairs = fetched.reshape(3, NPNO, NPNO).astype(jnp.float32)
    half = rounded(jnp.einsum('mpq,mqa->mpa', pairs, coverf))
    proj = rounded(jnp.einsum('mpa,mpd->mad', coverf, half))
    wparts = rounded(jnp.einsum('mad,gdbmc->gabc', proj, integrals))
    wsum = jnp.sum(wparts, axis=0)
    occ_sum = jnp.sum(occupied)
    denom = energy[:, None, None] + energy[None, :, None] + energy[None, None, :] - occ_sum + SHIFT_LEVEL
    keep = jnp.arange(NT) < rank
    mask = keep[:, None, None] & keep[None, :, None] & keep[None, None, :]
    fresh = jnp.where(mask, (SHIFT_LEVEL * amplitude.reshape(NT, NT, NT) + wsum) / denom, 0.0)
    fresh_half = rounded(fresh)
    resid = jnp.sum(jnp.einsum('abc,gdbmc->gmad', fresh_half, integrals), axis=0)
    left = jnp.einsum('mpa,mad->mpd', coverf, resid, precision=lax.Precision.HIGHEST)
    back = jnp.einsum('mpd,mqd->mpq', left, coverf, precision=lax.Precision.HIGHEST).astype(jnp.bfloat16)
    return fresh.reshape(NT, NT * NT), back.reshape(3, NPNO * NPNO)


def reference(aux_blocks, occ_blocks, intersections, tno_energy, occ_energy, tno_rank, triples_old, pair_amps, pno_energy, pair_occ, pair_rank, request_owner, request_row):
    pair_ids = (request_owner[:, :, 0] * PAIRS_DEV + request_row).astype(jnp.int32)
    npairs = pair_amps.shape[0]
    live = jnp.arange(NPNO)[None, :] < pair_rank[:, None]
    pair_keep = (live[:, :, None] & live[:, None, :]).reshape(npairs, NPNO * NPNO)
    denom = (pno_energy[:, :, None] + pno_energy[:, None, :] + pair_occ[:, None, None] + SHIFT_LEVEL).reshape(npairs, NPNO * NPNO)
    amps = pair_amps.astype(jnp.float32)
    state = triples_old
    for step in range(PASSES):
        masked = jnp.where(pair_keep, amps.astype(jnp.bfloat16), jnp.zeros((), jnp.bfloat16))
        fetched = masked[pair_ids]
        state, back = lax.map(one_triple, (aux_blocks, occ_blocks, intersections, tno_energy, occ_energy, tno_rank, state, fetched))
        total = jnp.zeros((npairs, NPNO * NPNO), jnp.float32).at[pair_ids.reshape(-1)].add(back.reshape(-1, NPNO * NPNO).astype(jnp.float32))
        amps = amps + jnp.where(pair_keep, total / denom, 0.0)
    return state, amps
```

```python
import jax
import jax.numpy as jnp
from jax import lax
from jax.sharding import PartitionSpec as P

PASSES = 2
SHIFT_LEVEL = 1.0
BF = jnp.bfloat16
F32 = jnp.float32


def mm(x, y):
    return jnp.dot(x, y, preferred_element_type=F32)


def swap(x, axis):
    return lax.all_to_all(x, axis, split_axis=0, concat_axis=0, tiled=True)


def integral_blocks(aux_blocks, occ_blocks):
    naux = lax.axis_size("aux")
    tdev, _, nsq = aux_blocks.shape
    ntno = occ_blocks.shape[2] // 3
    full = jnp.einsum(
        "tqx,tqy->txy", aux_blocks, occ_blocks, preferred_element_type=F32
    ).astype(BF)
    last = full[naux].reshape(ntno, naux, ntno // naux, 3 * ntno).transpose(1, 2, 0, 3)
    last = last.reshape(naux, nsq // naux, 3 * ntno)
    return jnp.concatenate([full[:naux], last], axis=1)


def integral_matrix(rows, ntno, share):
    nsq = ntno * ntno
    own = rows[:nsq].reshape(ntno, ntno, 3, ntno).transpose(2, 0, 1, 3).reshape(3 * ntno, nsq)
    last = rows[nsq:].reshape(share, ntno, 3, ntno).transpose(2, 1, 0, 3)
    return own, last.reshape(3 * ntno, share * ntno)


def body(
    aux_blocks,
    occ_blocks,
    intersections,
    tno_energy,
    occ_energy,
    tno_rank,
    triples_old,
    pair_amps,
    pno_energy,
    pair_occ,
    pair_rank,
    request_owner,
    request_row,
):
    tdev = aux_blocks.shape[0]
    ntno = tno_energy.shape[1]
    npno = pno_energy.shape[1]
    pdev = pair_amps.shape[0]
    naux = lax.axis_size("aux")
    ntrip = lax.axis_size("trip")
    member = lax.axis_index("aux")
    share = ntno // naux
    nreq = 3 * tdev
    nsq = ntno * ntno
    prow = npno // naux
    chunk = prow * npno // 128
    owner = request_owner.reshape(nreq)
    local = request_row.reshape(nreq)

    placed = owner[:, None] == jnp.arange(ntrip)[None, :]
    wanted = jnp.sum(jnp.where(placed, local[:, None] + 1, 0), axis=0) - 1
    asked = swap(wanted.reshape(ntrip, 1), "trip")

    rows = lax.psum_scatter(
        integral_blocks(aux_blocks, occ_blocks), "aux", scatter_dimension=0, tiled=True
    )[0]

    number = jnp.arange(naux * 6 * chunk)
    dest, k, piece = number // (6 * chunk), (number // chunk) % 6, number % chunk
    request = jnp.where(k < 3, 3 * dest + k, 3 * naux + k - 3)
    req_owner = jnp.sum(
        jnp.where(request[:, None] == jnp.arange(nreq)[None, :], owner[None, :], 0), axis=1
    )
    column = jnp.arange(ntrip * chunk)
    route = (req_owner * chunk + piece)[:, None] == column[None, :]
    route = route.astype(BF)
    route_back = route.T
    own_rows = jnp.arange(pdev * chunk)
    serve = (asked * chunk + jnp.arange(chunk)[None, :]).reshape(ntrip * chunk)
    serve = jnp.where(jnp.repeat(asked.reshape(ntrip) >= 0, chunk), serve, -1)
    serve = (serve[:, None] == own_rows[None, :]).astype(BF)
    serve_back = serve.T

    live = jnp.arange(npno)[None, :] < pair_rank[:, None]
    live_p = lax.dynamic_slice_in_dim(live, member * prow, prow, 1)
    energy_p = lax.dynamic_slice_in_dim(pno_energy, member * prow, prow, 1)
    pair_keep = (live_p[:, :, None] & live[:, None, :]).reshape(pdev * chunk, 128)
    pair_den = (
        energy_p[:, :, None] + pno_energy[:, None, :] + pair_occ[:, None, None] + SHIFT_LEVEL
    ).reshape(pdev * chunk, 128)
    amps = (
        lax.dynamic_slice_in_dim(pair_amps, member * prow * npno, prow * npno, 1)
        .reshape(pdev * chunk, 128)
        .astype(F32)
    )
    gain = jnp.zeros_like(amps)

    def two(x):
        return lax.dynamic_slice_in_dim(x, member, 1, 0)[0], x[naux]

    old = triples_old.astype(BF)
    old_last = old[naux].reshape(share, naux, share * ntno).transpose(1, 0, 2)
    old = swap(jnp.concatenate([old[:naux], old_last], axis=2), "aux")
    old = old.reshape(ntno, nsq + share * ntno).astype(F32)
    states = [old[:, :nsq], old[:, nsq:]]
    energies, sums, ranks, covers = (
        two(tno_energy),
        two(jnp.sum(occ_energy, axis=1)),
        two(tno_rank),
        two(intersections),
    )
    dens, keeps = [], []
    for which in range(2):
        e, low = energies[which], 0
        live_t = jnp.arange(ntno) < ranks[which]
        e_b, live_b = e, live_t
        if which == 1:
            e_b = lax.dynamic_slice_in_dim(e, member * share, share, 0)
            live_b = lax.dynamic_slice_in_dim(live_t, member * share, share, 0)
        den = e[:, None, None] + e_b[None, :, None] + e[None, None, :] - sums[which] + SHIFT_LEVEL
        keep = live_t[:, None, None] & live_b[None, :, None] & live_t[None, None, :]
        dens.append(den.reshape(ntno, -1))
        keeps.append(keep.reshape(ntno, -1))
    matrices = integral_matrix(rows, ntno, share)

    for step in range(PASSES):
        outgoing = jnp.where(pair_keep, amps.astype(BF), jnp.zeros((), BF))
        found = mm(serve, outgoing).astype(BF).reshape(ntrip, chunk, 128)
        arrived = swap(found, "trip").reshape(ntrip * chunk, 128)
        handed = mm(route, arrived).astype(BF).reshape(naux, 6 * chunk, 128)
        fetched = swap(handed, "aux").reshape(naux, 6, prow, npno)
        fetched = fetched.transpose(1, 0, 2, 3).reshape(2, 3, npno, npno)
        backs = []
        for which in range(2):
            cover = covers[which]
            half = jnp.einsum(
                "mpq,mqa->mpa", fetched[which], cover, preferred_element_type=F32
            ).astype(BF)
            proj = jnp.einsum("mpa,mpd->amd", cover, half, preferred_element_type=F32)
            proj = proj.astype(BF).reshape(ntno, 3 * ntno)
            w = mm(proj, matrices[which])
            state = jnp.where(keeps[which], (SHIFT_LEVEL * states[which] + w) / dens[which], 0.0)
            states[which] = state
            resid = jnp.einsum(
                "an,xn->ax", state.astype(BF), matrices[which], preferred_element_type=F32
            ).reshape(ntno, 3, ntno)
            cover = cover.astype(F32)
            left = jnp.einsum("mpa,amd->mpd", cover, resid, precision=lax.Precision.HIGHEST)
            back = jnp.einsum("mpd,mqd->mpq", left, cover, precision=lax.Precision.HIGHEST)
            backs.append(back.astype(BF))
        back = jnp.stack(backs).reshape(6, naux, chunk, 128).transpose(1, 0, 2, 3)
        came = swap(back.reshape(naux, 6 * chunk, 128), "aux").reshape(naux * 6 * chunk, 128)
        sent = mm(route_back, came).astype(BF).reshape(ntrip, chunk, 128)
        came = swap(sent, "trip").reshape(ntrip * chunk, 128)
        total = mm(serve_back, came)
        change = jnp.where(pair_keep, total / pair_den, 0.0)
        gain = gain + change
        amps = amps + change

    new = jnp.concatenate(states, axis=1).reshape(naux, share, nsq + share * ntno)
    new = swap(new.astype(BF), "aux").astype(F32)
    last = new[:, :, nsq:].transpose(1, 0, 2).reshape(1, share, nsq)
    triples_new = jnp.concatenate([new[:, :, :nsq], last], axis=0)
    gains = jnp.broadcast_to(gain.astype(BF)[None], (naux, pdev * chunk, 128))
    gains = swap(gains, "aux").reshape(naux, pdev, prow * npno).transpose(1, 0, 2)
    pairs_new = pair_amps.astype(F32) + gains.reshape(pdev, npno * npno).astype(F32)
    return triples_new, pairs_new


def solution(mesh):
    in_specs = (
        P("trip", "aux", None),
        P("trip", "aux", None),
        P("trip", None, None, None),
        P("trip", None),
        P("trip", None),
        P("trip"),
        P("trip", "aux", None),
        P("trip", None),
        P("trip", None),
        P("trip"),
        P("trip"),
        P("trip", None, None),
        P("trip", None),
    )
    out_specs = (P("trip", "aux", None), P("trip", None))
    return jax.shard_map(body, mesh=mesh, in_specs=in_specs, out_specs=out_specs, check_vma=False)
```

```python
import jax
import jax.numpy as jnp
from jax import lax
from jax.sharding import PartitionSpec as P

PASSES = 2
SHIFT_LEVEL = 1.0
BF = jnp.bfloat16
F32 = jnp.float32


def mm(x, y):
    return jnp.dot(x, y, preferred_element_type=F32)


def swap(x, axis):
    return lax.all_to_all(x, axis, split_axis=0, concat_axis=0, tiled=True)


def integral_blocks(aux_blocks, occ_blocks):
    naux = lax.axis_size("aux")
    nsq = aux_blocks.shape[2]
    ntno = occ_blocks.shape[2] // 3
    share = ntno // naux
    full = jnp.einsum(
        "tqy,tqx->tyx", occ_blocks, aux_blocks, preferred_element_type=F32
    ).astype(BF)
    last = full[naux].reshape(3, naux, share, nsq).transpose(1, 0, 2, 3)
    last = last.reshape(naux, 3 * share, nsq)
    both = jnp.concatenate([full[:naux], last], axis=1)
    return jnp.pad(both, ((0, 0), (0, -both.shape[1] % 16), (0, -nsq % 128)))


def integral_matrix(rows, ntno, share):
    nsq = ntno * ntno
    rows = rows[: 3 * (ntno + share), :nsq].reshape(3 * (ntno + share), ntno, ntno)
    own = rows[: 3 * ntno].reshape(3, ntno, ntno, ntno).transpose(0, 2, 3, 1)
    last = rows[3 * ntno :].reshape(3, share, ntno, ntno).transpose(0, 2, 3, 1)
    return own.reshape(3 * ntno, nsq), last.reshape(3 * ntno, share * ntno)


def body(
    aux_blocks,
    occ_blocks,
    intersections,
    tno_energy,
    occ_energy,
    tno_rank,
    triples_old,
    pair_amps,
    pno_energy,
    pair_occ,
    pair_rank,
    request_owner,
    request_row,
):
    tdev = aux_blocks.shape[0]
    ntno = tno_energy.shape[1]
    npno = pno_energy.shape[1]
    pdev = pair_amps.shape[0]
    naux = lax.axis_size("aux")
    ntrip = lax.axis_size("trip")
    member = lax.axis_index("aux")
    share = ntno // naux
    nreq = 3 * tdev
    nsq = ntno * ntno
    prow = npno // naux
    chunk = prow * npno // 128
    owner = request_owner.reshape(nreq)
    local = request_row.reshape(nreq)

    placed = owner[:, None] == jnp.arange(ntrip)[None, :]
    wanted = jnp.sum(jnp.where(placed, local[:, None] + 1, 0), axis=0) - 1
    blocks, wanted = lax.optimization_barrier((integral_blocks(aux_blocks, occ_blocks), wanted))
    rows = lax.psum_scatter(blocks, "aux", scatter_dimension=0, tiled=True)[0]
    asked = swap(wanted.reshape(ntrip, 1), "trip")

    number = jnp.arange(naux * 6 * chunk)
    dest, k, piece = number // (6 * chunk), (number // chunk) % 6, number % chunk
    request = jnp.where(k < 3, 3 * dest + k, 3 * naux + k - 3)
    req_owner = jnp.sum(
        jnp.where(request[:, None] == jnp.arange(nreq)[None, :], owner[None, :], 0), axis=1
    )
    column = jnp.arange(ntrip * chunk)
    route = (req_owner * chunk + piece)[:, None] == column[None, :]
    route = route.astype(BF)
    route_back = route.T
    own_rows = jnp.arange(pdev * chunk)
    serve = (asked * chunk + jnp.arange(chunk)[None, :]).reshape(ntrip * chunk)
    serve = jnp.where(jnp.repeat(asked.reshape(ntrip) >= 0, chunk), serve, -1)
    serve = (serve[:, None] == own_rows[None, :]).astype(BF)
    serve_back = serve.T

    live = jnp.arange(npno)[None, :] < pair_rank[:, None]
    live_p = lax.dynamic_slice_in_dim(live, member * prow, prow, 1)
    energy_p = lax.dynamic_slice_in_dim(pno_energy, member * prow, prow, 1)
    pair_keep = (live_p[:, :, None] & live[:, None, :]).reshape(pdev * chunk, 128)
    pair_den = (
        energy_p[:, :, None] + pno_energy[:, None, :] + pair_occ[:, None, None] + SHIFT_LEVEL
    ).reshape(pdev * chunk, 128)
    amps = (
        lax.dynamic_slice_in_dim(pair_amps, member * prow * npno, prow * npno, 1)
        .reshape(pdev * chunk, 128)
        .astype(F32)
    )
    gain = jnp.zeros_like(amps)

    def two(x):
        return lax.dynamic_slice_in_dim(x, member, 1, 0)[0], x[naux]

    old = triples_old.astype(BF)
    old_last = old[naux].reshape(share, ntno, naux, share).transpose(2, 0, 1, 3)
    old_last = old_last.reshape(naux, share, ntno * share)
    old = swap(jnp.concatenate([old[:naux], old_last], axis=2), "aux")
    old = old.reshape(ntno, nsq + share * ntno).astype(F32)
    states = [old[:, :nsq], old[:, nsq:]]
    energies, sums, ranks, covers = (
        two(tno_energy),
        two(jnp.sum(occ_energy, axis=1)),
        two(tno_rank),
        two(intersections),
    )
    dens, keeps = [], []
    for which in range(2):
        e = energies[which]
        live_t = jnp.arange(ntno) < ranks[which]
        e_c, live_c = e, live_t
        if which == 1:
            e_c = lax.dynamic_slice_in_dim(e, member * share, share, 0)
            live_c = lax.dynamic_slice_in_dim(live_t, member * share, share, 0)
        den = e[:, None, None] + e[None, :, None] + e_c[None, None, :] - sums[which] + SHIFT_LEVEL
        keep = live_t[:, None, None] & live_t[None, :, None] & live_c[None, None, :]
        dens.append(den.reshape(ntno, -1))
        keeps.append(keep.reshape(ntno, -1))
    matrices = integral_matrix(rows, ntno, share)

    for step in range(PASSES):
        outgoing = jnp.where(pair_keep, amps.astype(BF), jnp.zeros((), BF))
        found = mm(serve, outgoing).astype(BF).reshape(ntrip, chunk, 128)
        arrived = swap(found, "trip").reshape(ntrip * chunk, 128)
        handed = mm(route, arrived).astype(BF).reshape(naux, 6 * chunk, 128)
        fetched = swap(handed, "aux").reshape(naux, 6, prow, npno)
        fetched = fetched.transpose(1, 0, 2, 3).reshape(2, 3, npno, npno)
        backs = []
        for which in range(2):
            cover = covers[which]
            half = jnp.einsum(
                "mpq,mqa->mpa", fetched[which], cover, preferred_element_type=F32
            ).astype(BF)
            proj = jnp.einsum("mpa,mpd->amd", cover, half, preferred_element_type=F32)
            proj = proj.astype(BF).reshape(ntno, 3 * ntno)
            w = mm(proj, matrices[which])
            state = jnp.where(keeps[which], (SHIFT_LEVEL * states[which] + w) / dens[which], 0.0)
            states[which] = state
            resid = jnp.einsum(
                "an,xn->ax", state.astype(BF), matrices[which], preferred_element_type=F32
            ).reshape(ntno, 3, ntno)
            cover = cover.astype(F32)
            left = jnp.einsum("mpa,amd->mpd", cover, resid, precision=lax.Precision.HIGHEST)
            back = jnp.einsum("mpd,mqd->mpq", left, cover, precision=lax.Precision.HIGHEST)
            backs.append(back.astype(BF))
        back = jnp.stack(backs).reshape(6, naux, chunk, 128).transpose(1, 0, 2, 3)
        came = swap(back.reshape(naux, 6 * chunk, 128), "aux").reshape(naux * 6 * chunk, 128)
        sent = mm(route_back, came).astype(BF).reshape(ntrip, chunk, 128)
        came = swap(sent, "trip").reshape(ntrip * chunk, 128)
        total = mm(serve_back, came)
        change = jnp.where(pair_keep, total / pair_den, 0.0)
        gain = gain + change
        amps = amps + change

    new = jnp.concatenate(states, axis=1).astype(BF)
    new = lax.all_gather(new, "aux", axis=0, tiled=False)
    new = lax.dynamic_slice_in_dim(new, member * share, share, 1).astype(F32)
    last = new[:, :, nsq:].reshape(naux, share, ntno, share).transpose(1, 2, 0, 3)
    triples_new = jnp.concatenate([new[:, :, :nsq], last.reshape(1, share, nsq)], axis=0)
    gains = jnp.broadcast_to(gain.astype(BF)[None], (naux, pdev * chunk, 128))
    gains = swap(gains, "aux").reshape(naux, pdev, prow * npno).transpose(1, 0, 2)
    pairs_new = pair_amps.astype(F32) + gains.reshape(pdev, npno * npno).astype(F32)
    return triples_new, pairs_new


def solution(mesh):
    in_specs = (
        P("trip", "aux", None),
        P("trip", "aux", None),
        P("trip", None, None, None),
        P("trip", None),
        P("trip", None),
        P("trip"),
        P("trip", "aux", None),
        P("trip", None),
        P("trip", None),
        P("trip"),
        P("trip"),
        P("trip", None, None),
        P("trip", None),
    )
    out_specs = (P("trip", "aux", None), P("trip", None))
    return jax.shard_map(body, mesh=mesh, in_specs=in_specs, out_specs=out_specs, check_vma=False)
```

```python
import functools
import jax
import jax.numpy as jnp
from jax import lax
from jax.experimental import pallas as pl
from jax.experimental.pallas import tpu as pltpu
from jax.sharding import PartitionSpec as P

PASSES = 2
SHIFT_LEVEL = 1.0
BF = jnp.bfloat16
F32 = jnp.float32
LANES = 128
VMEM_LIMIT = 48 * 2**20


def mm(x, y):
    return jnp.dot(x, y, preferred_element_type=F32)


def mm_nt(x, y):
    return lax.dot_general(x, y, (((1,), (1,)), ((), ())), preferred_element_type=F32)


def mm_tn(x, y):
    return lax.dot_general(x, y, (((0,), (0,)), ((), ())), preferred_element_type=F32)


def high_low(x):
    high = x.astype(BF)
    return high, (x - high.astype(F32)).astype(BF)


def swap(x, axis):
    return lax.all_to_all(x, axis, split_axis=0, concat_axis=0, tiled=True)


def up(n, m):
    return -(-n // m) * m


def call(kernel, outs, scratch=()):
    return pl.pallas_call(
        kernel,
        out_shape=outs,
        scratch_shapes=list(scratch),
        compiler_params=pltpu.CompilerParams(vmem_limit_bytes=VMEM_LIMIT),
    )


def blocks_kernel(naux, share, aux_ref, occ_ref, out_ref, last_ref):
    nsq, depth = aux_ref.shape[1:]
    width = occ_ref.shape[1]
    ntno = share * naux
    for t in range(0, naux, 2):
        left = jnp.concatenate([aux_ref[t], aux_ref[t + 1]], axis=1)
        none = jnp.zeros((LANES - width, depth), BF)
        zero = jnp.zeros((LANES, depth), BF)
        first = jnp.concatenate([occ_ref[t], none, zero], axis=0)
        second = jnp.concatenate([zero, occ_ref[t + 1], none], axis=0)
        right = jnp.concatenate([first, second], axis=1)
        both = mm_nt(left, right).astype(BF)
        out_ref[t, :nsq, :] = both[:, :LANES]
        out_ref[t + 1, :nsq, :] = both[:, LANES:]
    none = jnp.zeros((LANES - width, depth), BF)
    last_ref[...] = mm_nt(aux_ref[naux], jnp.concatenate([occ_ref[naux], none], axis=0))
    rest = out_ref.shape[1] - nsq - share * ntno
    for member in range(naux):
        parts = [
            last_ref[pl.ds(member * share + b, ntno, stride=ntno), :] for b in range(share)
        ]
        parts.append(jnp.zeros((rest, LANES), F32))
        out_ref[member, nsq:, :] = jnp.concatenate(parts, axis=0).astype(BF)


def integral_blocks(aux_blocks, occ_blocks, naux):
    _, depth, nsq = aux_blocks.shape
    ntno = occ_blocks.shape[2] // 3
    share = ntno // naux
    rows = up(nsq + share * ntno, 16)
    return call(
        functools.partial(blocks_kernel, naux, share),
        jax.ShapeDtypeStruct((naux, rows, LANES), BF),
        [pltpu.VMEM((nsq, LANES), F32)],
    )(aux_blocks.transpose(0, 2, 1), occ_blocks.transpose(0, 2, 1))


def pack_kernel(naux, route_ref, arrived_ref, old_ref, out_ref):
    share, nsq = old_ref.shape[1:]
    slab = nsq // naux
    part = out_ref.shape[0] // naux
    handed = mm(route_ref[...], arrived_ref[...]).astype(BF)
    pieces = handed.shape[0] // out_ref.shape[0]
    span = out_ref.shape[1] - pieces * LANES
    for x in range(pieces):
        out_ref[:, span + x * LANES : span + (x + 1) * LANES] = handed[
            x * out_ref.shape[0] : (x + 1) * out_ref.shape[0]
        ]
    rows = []
    for member in range(naux):
        row = jnp.concatenate(
            [
                old_ref[member],
                jnp.zeros((share, LANES * (nsq // LANES + 1) - nsq), F32),
                old_ref[naux][:, member * slab : (member + 1) * slab],
                jnp.zeros((share, span - LANES * (nsq // LANES + 1) - slab), F32),
            ],
            axis=1,
        )
        rows.append(jnp.concatenate([row, jnp.zeros((part - share, span), F32)], axis=0))
    out_ref[:, :span] = jnp.concatenate(rows, axis=0).astype(BF)


def block_mask(rows, row_block, cols, col_block):
    row = lax.broadcasted_iota(jnp.int32, (rows, cols), 0) // row_block
    return row == lax.broadcasted_iota(jnp.int32, (rows, cols), 1) // col_block


def fetch_order(naux, chunk, first):
    size = naux * 6 * chunk
    here = lax.broadcasted_iota(jnp.int32, (size, size), 0)
    there = lax.broadcasted_iota(jnp.int32, (size, size), 1)
    k, source, piece = here // (naux * chunk), (here // chunk) % naux, here % chunk
    if first:
        part = 6 * chunk // 3
        at = k * chunk + piece
        spot = (at // part) * (naux * part) + source * part + at % part
    else:
        spot = source * 6 * chunk + k * chunk + piece
    return (spot == there).astype(BF)


def triple_work(naux, chunk, ordered, covers, pieces, state, col, row, matrix):
    ntno = matrix.shape[0] // 3
    npno = covers.shape[1]
    half_rows = naux * chunk
    stack = []
    for k in range(3):
        block = ordered[k * half_rows : (k + 1) * half_rows]
        stack += [block[:, :npno], block[:, npno:]]
    stack = jnp.concatenate(stack, axis=0).astype(BF)
    mask = block_mask(3 * npno, npno, 3 * ntno, ntno)
    half = jnp.where(mask, mm_nt(stack, covers), 0.0).astype(BF)
    proj = mm_tn(pieces, half).astype(BF)
    state = (SHIFT_LEVEL * state + mm(proj, matrix)) / (col + row)
    resid = mm_nt(state.astype(BF), matrix)
    high, low = high_low(resid)
    left = jnp.where(mask, mm(pieces, high) + mm(pieces, low), 0.0)
    high, low = high_low(left)
    back = mm(high, covers) + mm(low, covers)
    packed = []
    for k in range(3):
        block = back[2 * k * half_rows : 2 * (k + 1) * half_rows]
        packed.append(jnp.concatenate([block[:half_rows], block[half_rows:]], axis=1))
    return state, jnp.concatenate(packed, axis=0)


def both_triples(naux, chunk, order, came, cover_ref, piece_ref, col_ref, row_ref, states, mats):
    ordered = mm(order, came)
    wide = mats[0].shape[1]
    rows = ordered.shape[0] // 2
    start = up(wide, LANES)
    new, sent = [], []
    for which in range(2):
        low, high = (0, wide) if which == 0 else (start, start + mats[1].shape[1])
        state, back = triple_work(
            naux,
            chunk,
            ordered[which * rows : (which + 1) * rows],
            cover_ref[which],
            piece_ref[which],
            states[which],
            col_ref[which],
            row_ref[:, low:high],
            mats[which],
        )
        new.append(state)
        sent.append(back)
    return new, jnp.concatenate(sent, axis=0).astype(BF)


def first_kernel(
    naux,
    chunk,
    came_ref,
    rows_ref,
    cover_ref,
    piece_ref,
    col_ref,
    row_ref,
    sent_ref,
    own_ref,
    last_ref,
    own_mat_ref,
    last_mat_ref,
    wide_ref,
):
    ntno, nsq = own_ref.shape
    share = ntno // naux
    wide_ref[...] = rows_ref[...].astype(F32)
    own = [wide_ref[pl.ds(b, ntno, stride=ntno), :] for b in range(ntno)]
    last = [wide_ref[pl.ds(nsq + b * ntno, ntno), :] for b in range(share)]
    for parts, out in ((own, own_mat_ref), (last, last_mat_ref)):
        out[...] = jnp.concatenate(
            [
                jnp.concatenate([x[:, m * ntno : (m + 1) * ntno] for x in parts], axis=1)
                for m in range(3)
            ],
            axis=0,
        ).astype(BF)
    came = came_ref[...]
    size = came.shape[0]
    span = came.shape[1] - 3 * LANES
    part = size // naux
    a = lax.broadcasted_iota(jnp.int32, (ntno, size), 0)
    there = lax.broadcasted_iota(jnp.int32, (ntno, size), 1)
    old = mm(((a // share) * part + a % share == there).astype(BF), came[:, :span])
    start = up(nsq, LANES)
    fetched = jnp.concatenate(
        [came[:, span + x * LANES : span + (x + 1) * LANES] for x in range(3)], axis=0
    )
    new, sent = both_triples(
        naux,
        chunk,
        fetch_order(naux, chunk, True),
        fetched,
        cover_ref,
        piece_ref,
        col_ref,
        row_ref,
        (old[:, :nsq], old[:, start : start + share * ntno]),
        (own_mat_ref[...], last_mat_ref[...]),
    )
    own_ref[...] = new[0]
    last_ref[...] = new[1]
    sent_ref[...] = mm_tn(fetch_order(naux, chunk, False), sent).astype(BF)


def later_kernel(
    naux,
    chunk,
    came_ref,
    cover_ref,
    piece_ref,
    col_ref,
    row_ref,
    own_ref,
    last_ref,
    own_mat_ref,
    last_mat_ref,
    sent_ref,
    new_ref,
):
    nsq = own_ref.shape[1]
    order = fetch_order(naux, chunk, False)
    new, sent = both_triples(
        naux,
        chunk,
        order,
        came_ref[...],
        cover_ref,
        piece_ref,
        col_ref,
        row_ref,
        (own_ref[...], last_ref[...]),
        (own_mat_ref[...], last_mat_ref[...]),
    )
    start, slab = up(nsq, LANES), last_ref.shape[1]
    new_ref[:, :nsq] = new[0].astype(BF)
    new_ref[:, start : start + slab] = new[1].astype(BF)
    sent_ref[...] = mm_tn(order, sent).astype(BF)


def body(
    aux_blocks,
    occ_blocks,
    intersections,
    tno_energy,
    occ_energy,
    tno_rank,
    triples_old,
    pair_amps,
    pno_energy,
    pair_occ,
    pair_rank,
    request_owner,
    request_row,
):
    tdev = aux_blocks.shape[0]
    ntno = tno_energy.shape[1]
    npno = pno_energy.shape[1]
    pdev = pair_amps.shape[0]
    naux = lax.axis_size("aux")
    ntrip = lax.axis_size("trip")
    member = lax.axis_index("aux")
    share = ntno // naux
    nreq = 3 * tdev
    nsq = ntno * ntno
    slab = share * ntno
    start = up(nsq, LANES)
    span = start + up(slab, LANES)
    prow = npno // naux
    chunk = prow * npno // LANES
    slots = ntrip * chunk
    owner = request_owner.reshape(nreq)
    local = request_row.reshape(nreq)

    slot = jnp.arange(ntrip)
    wanted = jnp.sum(
        jnp.where(owner[:, None] == slot[None, :], local[:, None] + 1, 0), axis=0
    ) - 1
    piece = jnp.arange(chunk)
    lane = jnp.arange(LANES)
    asking = (wanted[:, None] * chunk + piece[None, :])[:, :, None] == lane[None, None, :]
    asking = (asking & (wanted >= 0)[:, None, None]).astype(BF)

    blocks = integral_blocks(aux_blocks, occ_blocks, naux)
    blocks, asking = lax.optimization_barrier((blocks, asking))
    rows = lax.psum_scatter(blocks, "aux", scatter_dimension=0, tiled=True)[0]
    serve = swap(asking, "trip").reshape(slots, LANES)

    def routing(dest, at):
        k, part = at // chunk, at % chunk
        request = jnp.where(k < 3, 3 * dest + k, 3 * naux + k - 3)
        asked = jnp.sum(
            jnp.where(request[:, None] == jnp.arange(nreq)[None, :], owner[None, :], 0), axis=1
        )
        return ((asked * chunk + part)[:, None] == jnp.arange(slots)[None, :]).astype(BF)

    number = jnp.arange(naux * 6 * chunk)
    route = routing(number // (6 * chunk), number % (6 * chunk))
    part = 6 * chunk // 3
    route_first = routing(
        (number // part) % naux, number // (naux * part) * part + number % part
    )
    route_back = route.T

    live = jnp.arange(npno)[None, :] < pair_rank[:, None]
    live_p = lax.dynamic_slice_in_dim(live, member * prow, prow, 1)
    energy_p = lax.dynamic_slice_in_dim(pno_energy, member * prow, prow, 1)
    pair_keep = (live_p[:, :, None] & live[:, None, :]).reshape(pdev * chunk, LANES)
    pair_den = (
        energy_p[:, :, None] + pno_energy[:, None, :] + pair_occ[:, None, None] + SHIFT_LEVEL
    ).reshape(pdev * chunk, LANES)
    amps = (
        lax.dynamic_slice_in_dim(pair_amps, member * prow * npno, prow * npno, 1)
        .reshape(pdev * chunk, LANES)
        .astype(F32)
    )
    gain = jnp.zeros_like(amps)

    def two(x):
        return jnp.stack([lax.dynamic_slice_in_dim(x, member, 1, 0)[0], x[naux]])

    energy = jnp.where(jnp.arange(ntno)[None, :] < tno_rank[:, None], tno_energy, jnp.inf)
    energy = two(energy)
    col = (energy - two(jnp.sum(occ_energy, axis=1))[:, None] + SHIFT_LEVEL)[:, :, None]
    energy_b = lax.dynamic_slice_in_dim(energy[1], member * share, share, 0)
    row = jnp.concatenate(
        [
            (energy[0][:, None] + energy[0][None, :]).reshape(nsq),
            jnp.zeros((start - nsq,), F32),
            (energy_b[:, None] + energy[1][None, :]).reshape(slab),
            jnp.zeros((span - start - slab,), F32),
        ]
    )[None, :]
    cover = two(intersections)
    flat = cover.transpose(0, 1, 3, 2).reshape(2, 3 * ntno, npno)
    split = cover.reshape(2, 3, npno // 2, 2, ntno).transpose(0, 1, 3, 2, 4)
    split = split.reshape(2, 3 * npno, ntno)

    for step in range(PASSES):
        outgoing = jnp.where(pair_keep, amps.astype(BF), jnp.zeros((), BF))
        pad = serve.shape[1] - outgoing.shape[0]
        found = mm(serve, jnp.pad(outgoing, ((0, pad), (0, 0)))).astype(BF)
        arrived = swap(found.reshape(ntrip, chunk, LANES), "trip").reshape(slots, LANES)
        if step == 0:
            packed = call(
                functools.partial(pack_kernel, naux),
                jax.ShapeDtypeStruct((naux * part, span + 3 * LANES), BF),
            )(route_first, arrived, triples_old)
            came = swap(packed.reshape(naux, part, span + 3 * LANES), "aux")
            sent, own, last, own_mat, last_mat = call(
                functools.partial(first_kernel, naux, chunk),
                (
                    jax.ShapeDtypeStruct((naux * 6 * chunk, LANES), BF),
                    jax.ShapeDtypeStruct((ntno, nsq), F32),
                    jax.ShapeDtypeStruct((ntno, slab), F32),
                    jax.ShapeDtypeStruct((3 * ntno, nsq), BF),
                    jax.ShapeDtypeStruct((3 * ntno, slab), BF),
                ),
                [pltpu.VMEM(rows.shape, F32)],
            )(came.reshape(naux * part, span + 3 * LANES), rows, flat, split, col, row)
        else:
            handed = mm(route, arrived).astype(BF).reshape(naux, 6 * chunk, LANES)
            came = swap(handed, "aux").reshape(naux * 6 * chunk, LANES)
            sent, new = call(
                functools.partial(later_kernel, naux, chunk),
                (
                    jax.ShapeDtypeStruct((naux * 6 * chunk, LANES), BF),
                    jax.ShapeDtypeStruct((ntno, span), BF),
                ),
            )(came, flat, split, col, row, own, last, own_mat, last_mat)
        came = swap(sent.reshape(naux, 6 * chunk, LANES), "aux")
        sent = mm(route_back, came.reshape(naux * 6 * chunk, LANES)).astype(BF)
        came = swap(sent.reshape(ntrip, chunk, LANES), "trip").reshape(slots, LANES)
        total = mm_tn(serve, came)[: pdev * chunk]
        change = jnp.where(pair_keep, total / pair_den, 0.0)
        gain = gain + change
        amps = amps + change

    new = lax.all_gather(new, "aux", axis=0, tiled=False)
    new = lax.dynamic_slice_in_dim(new, member * share, share, 1).astype(F32)
    last = new[:, :, start : start + slab].transpose(1, 0, 2).reshape(1, share, nsq)
    triples_new = jnp.concatenate([new[:, :, :nsq], last], axis=0)
    gains = jnp.broadcast_to(gain.astype(BF)[None], (naux, pdev * chunk, LANES))
    gains = swap(gains, "aux").reshape(naux, pdev, prow * npno).transpose(1, 0, 2)
    pairs_new = pair_amps.astype(F32) + gains.reshape(pdev, npno * npno).astype(F32)
    return triples_new, pairs_new


def solution(mesh):
    in_specs = (
        P("trip", "aux", None),
        P("trip", "aux", None),
        P("trip", None, None, None),
        P("trip", None),
        P("trip", None),
        P("trip"),
        P("trip", "aux", None),
        P("trip", None),
        P("trip", None),
        P("trip"),
        P("trip"),
        P("trip", None, None),
        P("trip", None),
    )
    out_specs = (P("trip", "aux", None), P("trip", None))
    return jax.shard_map(body, mesh=mesh, in_specs=in_specs, out_specs=out_specs, check_vma=False)
```

```python
import functools
import jax
import jax.numpy as jnp
from jax import lax
from jax.experimental import pallas as pl
from jax.experimental.pallas import tpu as pltpu
from jax.sharding import PartitionSpec as P

PASSES = 2
SHIFT_LEVEL = 1.0
BF = jnp.bfloat16
F32 = jnp.float32
LANES = 128
VMEM_LIMIT = 48 * 2**20
VMEM_ALL = 63 * 2**20


def mm(x, y):
    return jnp.dot(x, y, preferred_element_type=F32)


def mm_nt(x, y):
    return lax.dot_general(x, y, (((1,), (1,)), ((), ())), preferred_element_type=F32)


def mm_tn(x, y):
    return lax.dot_general(x, y, (((0,), (0,)), ((), ())), preferred_element_type=F32)


def high_low(x):
    high = x.astype(BF)
    return high, (x - high.astype(F32)).astype(BF)


def swap(x, axis):
    return lax.all_to_all(x, axis, split_axis=0, concat_axis=0, tiled=True)


def up(n, m):
    return -(-n // m) * m


def call(kernel, outs, scratch=(), limit=VMEM_LIMIT, **specs):
    return pl.pallas_call(
        kernel,
        out_shape=outs,
        scratch_shapes=list(scratch),
        **specs,
        compiler_params=pltpu.CompilerParams(vmem_limit_bytes=limit),
    )


def blocks_kernel(
    naux,
    share,
    aux_ref,
    occ_far_ref,
    owner_far_ref,
    local_far_ref,
    out_ref,
    asking_out_ref,
    held_ref,
    made_ref,
    last_ref,
    occ_ref,
    owner_ref,
    local_ref,
    asking_ref,
    in_sems,
    out_sems,
    more_sems,
):
    nsq, depth = held_ref.shape[1:]
    width = occ_ref.shape[1]
    ntno = share * naux
    groups = [naux // 2, 0]
    ends = [naux + 1, naux // 2]
    arriving = []
    for n, (t, end) in enumerate(zip(groups, ends)):
        part = pl.ds(t, end - t)
        copy = pltpu.make_async_copy(aux_ref.at[part], held_ref.at[part], in_sems.at[n])
        copy.start()
        arriving.append(copy)
    pairs = ((owner_far_ref, owner_ref), (local_far_ref, local_ref), (occ_far_ref, occ_ref))
    first = [pltpu.make_async_copy(x, y, more_sems.at[n]) for n, (x, y) in enumerate(pairs)]
    for copy in first:
        copy.start()
    for copy in first:
        copy.wait()
    chunk = asking_ref.shape[1]
    asking_ref[...] = jnp.zeros(asking_ref.shape, BF)
    piece = lax.broadcasted_iota(jnp.int32, (chunk, LANES), 0)
    lane = lax.broadcasted_iota(jnp.int32, (chunk, LANES), 1)
    for m in range(local_ref.shape[0]):
        for t in range(local_ref.shape[1]):
            hot = (lane == local_ref[m, t] * chunk + piece).astype(F32).astype(BF)
            asking_ref[pl.ds(owner_ref[m, 0, t], 1)] = hot[None]
    asked = pltpu.make_async_copy(asking_ref, asking_out_ref, more_sems.at[3])
    asked.start()

    none = jnp.zeros((LANES - width, depth), BF)
    zero = jnp.zeros((LANES, depth), BF)
    rest = made_ref.shape[1] - nsq - share * ntno
    leaving = []
    for n, (low, end) in enumerate(zip(groups, ends)):
        arriving[n].wait()
        if end > naux:
            right = jnp.concatenate([occ_ref[naux], none], axis=0)
            last_ref[...] = mm_nt(held_ref[naux], right)
        top = min(end, naux)
        for t in range(low, top, 2):
            left = jnp.concatenate([held_ref[t], held_ref[t + 1]], axis=1)
            upper = jnp.concatenate([occ_ref[t], none, zero], axis=0)
            lower = jnp.concatenate([zero, occ_ref[t + 1], none], axis=0)
            both = mm_nt(left, jnp.concatenate([upper, lower], axis=1)).astype(BF)
            made_ref[t, :nsq, :] = both[:, :LANES]
            made_ref[t + 1, :nsq, :] = both[:, LANES:]
            for member in (t, t + 1):
                parts = [
                    last_ref[pl.ds(member * share + b, ntno, stride=ntno), :]
                    for b in range(share)
                ]
                parts.append(jnp.zeros((rest, LANES), F32))
                made_ref[member, nsq:, :] = jnp.concatenate(parts, axis=0).astype(BF)
        part = pl.ds(low, top - low)
        copy = pltpu.make_async_copy(made_ref.at[part], out_ref.at[part], out_sems.at[n])
        copy.start()
        leaving.append(copy)
    for copy in leaving:
        copy.wait()
    asked.wait()


def integral_blocks(aux_blocks, occ_blocks, request_owner, request_row, naux, ntrip, chunk):
    tdev, depth, nsq = aux_blocks.shape
    ntno = occ_blocks.shape[2] // 3
    share = ntno // naux
    rows = up(nsq + share * ntno, 16)
    far = pl.BlockSpec(memory_space=pltpu.HBM)
    return call(
        functools.partial(blocks_kernel, naux, share),
        (
            jax.ShapeDtypeStruct((naux, rows, LANES), BF),
            jax.ShapeDtypeStruct((ntrip, chunk, LANES), BF),
        ),
        [
            pltpu.VMEM((tdev, nsq, depth), BF),
            pltpu.VMEM((naux, rows, LANES), BF),
            pltpu.VMEM((nsq, LANES), F32),
            pltpu.VMEM((tdev, occ_blocks.shape[2], depth), BF),
            pltpu.SMEM((3, 1, tdev), jnp.int32),
            pltpu.SMEM((3, tdev), jnp.int32),
            pltpu.VMEM((ntrip, chunk, LANES), BF),
            pltpu.SemaphoreType.DMA((2,)),
            pltpu.SemaphoreType.DMA((2,)),
            pltpu.SemaphoreType.DMA((4,)),
        ],
        VMEM_ALL,
        in_specs=[far] * 4,
        out_specs=(far, far),
    )(
        aux_blocks.transpose(0, 2, 1),
        occ_blocks.transpose(0, 2, 1),
        request_owner.transpose(1, 2, 0),
        request_row.T,
    )


def pack_kernel(naux, route_ref, arrived_ref, old_ref, out_ref):
    share, nsq = old_ref.shape[1:]
    slab = nsq // naux
    part = out_ref.shape[0] // naux
    handed = mm(route_ref[...], arrived_ref[...]).astype(BF)
    pieces = handed.shape[0] // out_ref.shape[0]
    span = out_ref.shape[1] - pieces * LANES
    for x in range(pieces):
        out_ref[:, span + x * LANES : span + (x + 1) * LANES] = handed[
            x * out_ref.shape[0] : (x + 1) * out_ref.shape[0]
        ]
    rows = []
    for member in range(naux):
        row = jnp.concatenate(
            [
                old_ref[member],
                jnp.zeros((share, LANES * (nsq // LANES + 1) - nsq), F32),
                old_ref[naux][:, member * slab : (member + 1) * slab],
                jnp.zeros((share, span - LANES * (nsq // LANES + 1) - slab), F32),
            ],
            axis=1,
        )
        rows.append(jnp.concatenate([row, jnp.zeros((part - share, span), F32)], axis=0))
    out_ref[:, :span] = jnp.concatenate(rows, axis=0).astype(BF)


def block_mask(rows, row_block, cols, col_block):
    row = lax.broadcasted_iota(jnp.int32, (rows, cols), 0) // row_block
    return row == lax.broadcasted_iota(jnp.int32, (rows, cols), 1) // col_block


def fetch_order(naux, chunk, first):
    size = naux * 6 * chunk
    here = jnp.arange(size)
    k, source, piece = here // (naux * chunk), (here // chunk) % naux, here % chunk
    if first:
        part = 6 * chunk // 3
        at = k * chunk + piece
        spot = (at // part) * (naux * part) + source * part + at % part
    else:
        spot = source * 6 * chunk + k * chunk + piece
    return (spot[:, None] == jnp.arange(size)[None, :]).astype(BF)


def project(naux, chunk, ordered, covers, pieces):
    npno, width = covers.shape[1], covers.shape[0]
    half_rows = naux * chunk
    stack = []
    for k in range(3):
        block = ordered[k * half_rows : (k + 1) * half_rows]
        stack += [block[:, :npno], block[:, npno:]]
    stack = jnp.concatenate(stack, axis=0).astype(BF)
    mask = block_mask(3 * npno, npno, width, width // 3)
    half = jnp.where(mask, mm_nt(stack, covers), 0.0).astype(BF)
    return mm_tn(pieces, half).astype(BF)


def residual(naux, chunk, new, covers, pieces, matrix):
    npno, width = covers.shape[1], covers.shape[0]
    half_rows = naux * chunk
    mask = block_mask(3 * npno, npno, width, width // 3)
    high, low = high_low(mm_nt(new, matrix))
    left = jnp.where(mask, mm(pieces, high) + mm(pieces, low), 0.0)
    high, low = high_low(left)
    back = mm(high, covers) + mm(low, covers)
    packed = []
    for k in range(3):
        block = back[2 * k * half_rows : 2 * (k + 1) * half_rows]
        packed.append(jnp.concatenate([block[:half_rows], block[half_rows:]], axis=1))
    return jnp.concatenate(packed, axis=0)


def project_both(naux, chunk, order, came, cover_ref, piece_ref):
    ordered = mm(order, came)
    rows = ordered.shape[0] // 2
    return [
        project(
            naux, chunk, ordered[w * rows : (w + 1) * rows], cover_ref[w], piece_ref[w]
        )
        for w in range(2)
    ]


def work_both(naux, chunk, projs, cover_ref, piece_ref, col_ref, row_ref, states, mats):
    wide = mats[0].shape[1]
    start = up(wide, LANES)
    spans = ((0, wide), (start, start + mats[1].shape[1]))
    new, sent = [], []
    for w in range(2):
        den = col_ref[w] + row_ref[:, spans[w][0] : spans[w][1]]
        new.append((SHIFT_LEVEL * states[w] + mm(projs[w], mats[w])) / den)
    halves = [x.astype(BF) for x in new]
    for w in range(2):
        sent.append(residual(naux, chunk, halves[w], cover_ref[w], piece_ref[w], mats[w]))
    return new, halves, jnp.concatenate(sent, axis=0).astype(BF)


def row_spots(ntno, naux, size):
    share, part = ntno // naux, size // naux
    a = lax.broadcasted_iota(jnp.int32, (ntno, size), 0)
    there = lax.broadcasted_iota(jnp.int32, (ntno, size), 1)
    return ((a // share) * part + a % share == there).astype(F32).astype(BF)


def relayout_kernel(ntno, share, rows_ref, own_ref, last_ref, wide_ref):
    nsq = ntno * ntno
    wide_ref[...] = rows_ref[...].astype(F32)
    own = [wide_ref[pl.ds(b, ntno, stride=ntno), :] for b in range(ntno)]
    last = [wide_ref[pl.ds(nsq + b * ntno, ntno), :] for b in range(share)]
    for parts, out in ((own, own_ref), (last, last_ref)):
        out[...] = jnp.concatenate(
            [
                jnp.concatenate([x[:, m * ntno : (m + 1) * ntno] for x in parts], axis=1)
                for m in range(3)
            ],
            axis=0,
        ).astype(BF)


def first_kernel(
    naux,
    chunk,
    came_ref,
    order_ref,
    later_order_ref,
    cover_ref,
    piece_ref,
    col_ref,
    row_ref,
    own_mat_ref,
    last_mat_ref,
    sent_ref,
    own_ref,
    last_ref,
):
    ntno, nsq = own_ref.shape
    slab = last_ref.shape[1]
    came = came_ref[...]
    size = came.shape[0]
    span = came.shape[1] - 3 * LANES
    start = up(nsq, LANES)
    fetched = jnp.concatenate(
        [came[:, span + x * LANES : span + (x + 1) * LANES] for x in range(3)], axis=0
    )
    projs = project_both(naux, chunk, order_ref[...], fetched, cover_ref, piece_ref)
    old = mm(row_spots(ntno, naux, size), came[:, :span])
    new, _, sent = work_both(
        naux,
        chunk,
        projs,
        cover_ref,
        piece_ref,
        col_ref,
        row_ref,
        (old[:, :nsq], old[:, start : start + slab]),
        (own_mat_ref[...], last_mat_ref[...]),
    )
    own_ref[...] = new[0]
    last_ref[...] = new[1]
    sent_ref[...] = mm_tn(later_order_ref[...], sent).astype(BF)


def later_kernel(
    naux,
    chunk,
    came_ref,
    order_ref,
    last_order_ref,
    cover_ref,
    piece_ref,
    col_ref,
    row_ref,
    own_ref,
    last_ref,
    own_mat_ref,
    last_mat_ref,
    out_ref,
    wide_ref,
):
    ntno, nsq = own_ref.shape
    size, width = out_ref.shape
    span = width - 3 * LANES
    start, slab = up(nsq, LANES), last_ref.shape[1]
    projs = project_both(naux, chunk, order_ref[...], came_ref[...], cover_ref, piece_ref)
    _, halves, sent = work_both(
        naux,
        chunk,
        projs,
        cover_ref,
        piece_ref,
        col_ref,
        row_ref,
        (own_ref[...], last_ref[...]),
        (own_mat_ref[...], last_mat_ref[...]),
    )
    wide_ref[...] = jnp.zeros(wide_ref.shape, BF)
    wide_ref[:, :nsq] = halves[0]
    wide_ref[:, start : start + slab] = halves[1]
    out_ref[:, :span] = mm_tn(row_spots(ntno, naux, size), wide_ref[...]).astype(BF)
    sent = mm_tn(last_order_ref[...], sent).astype(BF)
    for x in range(3):
        out_ref[:, span + x * LANES : span + (x + 1) * LANES] = sent[x * size : (x + 1) * size]


def finish_kernel(naux, came_ref, out_ref):
    share, nsq = out_ref.shape[1:]
    start, slab = up(nsq, LANES), nsq // naux
    part = came_ref.shape[0] // naux
    came = came_ref[:, : up(start + slab, LANES)].astype(F32)
    last = []
    for member in range(naux):
        rows = came[member * part : member * part + share]
        out_ref[member] = rows[:, :nsq]
        last.append(rows[:, start : start + slab])
    out_ref[naux] = jnp.concatenate(last, axis=1)


def body(
    aux_blocks,
    occ_blocks,
    intersections,
    tno_energy,
    occ_energy,
    tno_rank,
    triples_old,
    pair_amps,
    pno_energy,
    pair_occ,
    pair_rank,
    request_owner,
    request_row,
):
    tdev = aux_blocks.shape[0]
    ntno = tno_energy.shape[1]
    npno = pno_energy.shape[1]
    pdev = pair_amps.shape[0]
    naux = lax.axis_size("aux")
    ntrip = lax.axis_size("trip")
    member = lax.axis_index("aux")
    share = ntno // naux
    nreq = 3 * tdev
    nsq = ntno * ntno
    slab = share * ntno
    start = up(nsq, LANES)
    span = start + up(slab, LANES)
    prow = npno // naux
    chunk = prow * npno // LANES
    slots = ntrip * chunk
    owner = request_owner.reshape(nreq)

    blocks, asking = integral_blocks(
        aux_blocks, occ_blocks, request_owner, request_row, naux, ntrip, chunk
    )
    rows = lax.psum_scatter(blocks, "aux", scatter_dimension=0, tiled=True)[0]
    serve = swap(asking, "trip").reshape(slots, LANES)

    def routing(dest, at):
        k, part = at // chunk, at % chunk
        request = jnp.where(k < 3, 3 * dest + k, 3 * naux + k - 3)
        asked = jnp.sum(
            jnp.where(request[:, None] == jnp.arange(nreq)[None, :], owner[None, :], 0), axis=1
        )
        return ((asked * chunk + part)[:, None] == jnp.arange(slots)[None, :]).astype(BF)

    number = jnp.arange(naux * 6 * chunk)
    route = routing(number // (6 * chunk), number % (6 * chunk))
    part = 6 * chunk // 3
    route_first = routing(
        (number // part) % naux, number // (naux * part) * part + number % part
    )
    route_back, route_last = route.T, route_first.T
    order, order_first = fetch_order(naux, chunk, False), fetch_order(naux, chunk, True)

    live = jnp.arange(npno)[None, :] < pair_rank[:, None]
    live_p = lax.dynamic_slice_in_dim(live, member * prow, prow, 1)
    energy_p = lax.dynamic_slice_in_dim(pno_energy, member * prow, prow, 1)
    pair_keep = (live_p[:, :, None] & live[:, None, :]).reshape(pdev * chunk, LANES)
    pair_den = (
        energy_p[:, :, None] + pno_energy[:, None, :] + pair_occ[:, None, None] + SHIFT_LEVEL
    ).reshape(pdev * chunk, LANES)
    amps = (
        lax.dynamic_slice_in_dim(pair_amps, member * prow * npno, prow * npno, 1)
        .reshape(pdev * chunk, LANES)
        .astype(F32)
    )
    gain = jnp.zeros_like(amps)

    def two(x):
        return jnp.stack([lax.dynamic_slice_in_dim(x, member, 1, 0)[0], x[naux]])

    masked = jnp.where(jnp.arange(ntno)[None, :] < tno_rank[:, None], tno_energy, jnp.inf)
    energy = two(masked)
    col = two(masked - jnp.sum(occ_energy, axis=1)[:, None] + SHIFT_LEVEL)[:, :, None]
    energy_b = lax.dynamic_slice_in_dim(energy[1], member * share, share, 0)
    row = jnp.concatenate(
        [
            (energy[0][:, None] + energy[0][None, :]).reshape(nsq),
            jnp.zeros((start - nsq,), F32),
            (energy_b[:, None] + energy[1][None, :]).reshape(slab),
            jnp.zeros((span - start - slab,), F32),
        ]
    )[None, :]
    cover = two(intersections)
    flat = cover.transpose(0, 1, 3, 2).reshape(2, 3 * ntno, npno)
    split = cover.reshape(2, 3, npno // 2, 2, ntno).transpose(0, 1, 3, 2, 4)
    split = split.reshape(2, 3 * npno, ntno)

    ready = (
        (serve, route, route_first, route_back, route_last, order, order_first)
        + (pair_keep, pair_den, amps, flat, split, col, row)
    )
    serve, route, route_first, route_back, route_last, order, order_first, *ready = (
        lax.optimization_barrier(ready)
    )
    pair_keep, pair_den, amps, flat, split, col, row = ready
    width = span + 3 * LANES

    for step in range(PASSES):
        outgoing = jnp.where(pair_keep, amps.astype(BF), jnp.zeros((), BF))
        pad = serve.shape[1] - outgoing.shape[0]
        found = mm(serve, jnp.pad(outgoing, ((0, pad), (0, 0)))).astype(BF)
        arrived = swap(found.reshape(ntrip, chunk, LANES), "trip").reshape(slots, LANES)
        if step == 0:
            packed = call(
                functools.partial(pack_kernel, naux),
                jax.ShapeDtypeStruct((naux * part, width), BF),
            )(route_first, arrived, triples_old)
            came = swap(packed.reshape(naux, part, width), "aux")
        else:
            handed = mm(route, arrived).astype(BF).reshape(naux, 6 * chunk, LANES)
            came = swap(handed, "aux")
        if step == 0:
            own_mat, last_mat = call(
                functools.partial(relayout_kernel, ntno, share),
                (
                    jax.ShapeDtypeStruct((3 * ntno, nsq), BF),
                    jax.ShapeDtypeStruct((3 * ntno, slab), BF),
                ),
                [pltpu.VMEM(rows.shape, F32)],
            )(rows)
            sent, own, last = call(
                functools.partial(first_kernel, naux, chunk),
                (
                    jax.ShapeDtypeStruct((naux * 6 * chunk, LANES), BF),
                    jax.ShapeDtypeStruct((ntno, nsq), F32),
                    jax.ShapeDtypeStruct((ntno, slab), F32),
                ),
            )(
                came.reshape(-1, width),
                order_first,
                order,
                flat,
                split,
                col,
                row,
                own_mat,
                last_mat,
            )
            came = swap(sent.reshape(naux, 6 * chunk, LANES), "aux")
            sent = mm(route_back, came.reshape(naux * 6 * chunk, LANES))
        else:
            sent = call(
                functools.partial(later_kernel, naux, chunk),
                jax.ShapeDtypeStruct((naux * part, width), BF),
                [pltpu.VMEM((ntno, span), BF)],
            )(
                came.reshape(-1, LANES),
                order,
                order_first,
                flat,
                split,
                col,
                row,
                own,
                last,
                own_mat,
                last_mat,
            )
            came = swap(sent.reshape(naux, part, width), "aux").reshape(naux * part, width)
            triples_new = call(
                functools.partial(finish_kernel, naux),
                jax.ShapeDtypeStruct((tdev, share, nsq), F32),
            )(came)
            back = [came[:, span + x * LANES : span + (x + 1) * LANES] for x in range(3)]
            sent = mm(route_last, jnp.concatenate(back, axis=0))
        sent = sent.astype(BF).reshape(ntrip, chunk, LANES)
        came = swap(sent, "trip").reshape(slots, LANES)
        total = mm_tn(serve, came)[: pdev * chunk]
        change = jnp.where(pair_keep, total / pair_den, 0.0)
        gain = gain + change
        amps = amps + change

    gains = jnp.broadcast_to(gain.astype(BF)[None], (naux, pdev * chunk, LANES))
    gains = swap(gains, "aux").reshape(naux, pdev, prow * npno).transpose(1, 0, 2)
    pairs_new = pair_amps.astype(F32) + gains.reshape(pdev, npno * npno).astype(F32)
    return triples_new, pairs_new


def solution(mesh):
    in_specs = (
        P("trip", "aux", None),
        P("trip", "aux", None),
        P("trip", None, None, None),
        P("trip", None),
        P("trip", None),
        P("trip"),
        P("trip", "aux", None),
        P("trip", None),
        P("trip", None),
        P("trip"),
        P("trip"),
        P("trip", None, None),
        P("trip", None),
    )
    out_specs = (P("trip", "aux", None), P("trip", None))
    return jax.shard_map(body, mesh=mesh, in_specs=in_specs, out_specs=out_specs, check_vma=False)
```

```python
import functools
import jax
import jax.numpy as jnp
from jax import lax
from jax.experimental import pallas as pl
from jax.experimental.pallas import tpu as pltpu
from jax.sharding import PartitionSpec as P

PASSES = 2
SHIFT_LEVEL = 1.0
BF = jnp.bfloat16
F32 = jnp.float32
LANES = 128
VMEM_LIMIT = 48 * 2**20
VMEM_ALL = 63 * 2**20


def mm(x, y):
    return jnp.dot(x, y, preferred_element_type=F32)


def mm_nt(x, y):
    return lax.dot_general(x, y, (((1,), (1,)), ((), ())), preferred_element_type=F32)


def mm_tn(x, y):
    return lax.dot_general(x, y, (((0,), (0,)), ((), ())), preferred_element_type=F32)


def high_low(x):
    high = x.astype(BF)
    return high, (x - high.astype(F32)).astype(BF)


def swap(x, axis):
    return lax.all_to_all(x, axis, split_axis=0, concat_axis=0, tiled=True)


def up(n, m):
    return -(-n // m) * m


def call(kernel, outs, scratch=(), limit=VMEM_LIMIT, **specs):
    return pl.pallas_call(
        kernel,
        out_shape=outs,
        scratch_shapes=list(scratch),
        **specs,
        compiler_params=pltpu.CompilerParams(vmem_limit_bytes=limit),
    )


def blocks_kernel(
    naux,
    share,
    aux_ref,
    occ_far_ref,
    owner_far_ref,
    local_far_ref,
    out_ref,
    asking_out_ref,
    held_ref,
    made_ref,
    last_ref,
    occ_ref,
    owner_ref,
    local_ref,
    asking_ref,
    in_sems,
    out_sems,
    more_sems,
):
    nsq, depth = held_ref.shape[1:]
    width = occ_ref.shape[1]
    ntno = share * naux
    groups = [naux // 2, 0]
    ends = [naux + 1, naux // 2]
    arriving = []
    for n, (t, end) in enumerate(zip(groups, ends)):
        part = pl.ds(t, end - t)
        copy = pltpu.make_async_copy(aux_ref.at[part], held_ref.at[part], in_sems.at[n])
        copy.start()
        arriving.append(copy)
    pairs = ((owner_far_ref, owner_ref), (local_far_ref, local_ref), (occ_far_ref, occ_ref))
    first = [pltpu.make_async_copy(x, y, more_sems.at[n]) for n, (x, y) in enumerate(pairs)]
    for copy in first:
        copy.start()
    for copy in first:
        copy.wait()
    chunk = asking_ref.shape[1]
    asking_ref[...] = jnp.zeros(asking_ref.shape, BF)
    piece = lax.broadcasted_iota(jnp.int32, (chunk, LANES), 0)
    lane = lax.broadcasted_iota(jnp.int32, (chunk, LANES), 1)
    for m in range(local_ref.shape[0]):
        for t in range(local_ref.shape[1]):
            hot = (lane == local_ref[m, t] * chunk + piece).astype(F32).astype(BF)
            asking_ref[pl.ds(owner_ref[m, 0, t], 1)] = hot[None]
    asked = pltpu.make_async_copy(asking_ref, asking_out_ref, more_sems.at[3])
    asked.start()

    none = jnp.zeros((LANES - width, depth), BF)
    zero = jnp.zeros((LANES, depth), BF)
    rest = made_ref.shape[1] - nsq - share * ntno
    leaving = []
    for n, (low, end) in enumerate(zip(groups, ends)):
        arriving[n].wait()
        if end > naux:
            right = jnp.concatenate([occ_ref[naux], none], axis=0)
            last_ref[...] = mm_nt(held_ref[naux], right)
        top = min(end, naux)
        for t in range(low, top, 2):
            left = jnp.concatenate([held_ref[t], held_ref[t + 1]], axis=1)
            upper = jnp.concatenate([occ_ref[t], none, zero], axis=0)
            lower = jnp.concatenate([zero, occ_ref[t + 1], none], axis=0)
            both = mm_nt(left, jnp.concatenate([upper, lower], axis=1)).astype(BF)
            made_ref[t, :nsq, :] = both[:, :LANES]
            made_ref[t + 1, :nsq, :] = both[:, LANES:]
            for member in (t, t + 1):
                parts = [
                    last_ref[pl.ds(member * share + b, ntno, stride=ntno), :]
                    for b in range(share)
                ]
                parts.append(jnp.zeros((rest, LANES), F32))
                made_ref[member, nsq:, :] = jnp.concatenate(parts, axis=0).astype(BF)
        part = pl.ds(low, top - low)
        copy = pltpu.make_async_copy(made_ref.at[part], out_ref.at[part], out_sems.at[n])
        copy.start()
        leaving.append(copy)
    for copy in leaving:
        copy.wait()
    asked.wait()


def integral_blocks(aux_blocks, occ_blocks, request_owner, request_row, naux, ntrip, chunk):
    tdev, depth, nsq = aux_blocks.shape
    ntno = occ_blocks.shape[2] // 3
    share = ntno // naux
    rows = up(nsq + share * ntno, 16)
    far = pl.BlockSpec(memory_space=pltpu.HBM)
    return call(
        functools.partial(blocks_kernel, naux, share),
        (
            jax.ShapeDtypeStruct((naux, rows, LANES), BF),
            jax.ShapeDtypeStruct((ntrip, chunk, LANES), BF),
        ),
        [
            pltpu.VMEM((tdev, nsq, depth), BF),
            pltpu.VMEM((naux, rows, LANES), BF),
            pltpu.VMEM((nsq, LANES), F32),
            pltpu.VMEM((tdev, occ_blocks.shape[2], depth), BF),
            pltpu.SMEM((3, 1, tdev), jnp.int32),
            pltpu.SMEM((3, tdev), jnp.int32),
            pltpu.VMEM((ntrip, chunk, LANES), BF),
            pltpu.SemaphoreType.DMA((2,)),
            pltpu.SemaphoreType.DMA((2,)),
            pltpu.SemaphoreType.DMA((4,)),
        ],
        VMEM_ALL,
        in_specs=[far] * 4,
        out_specs=(far, far),
    )(
        aux_blocks.transpose(0, 2, 1),
        occ_blocks.transpose(0, 2, 1),
        request_owner.transpose(1, 2, 0),
        request_row.T,
    )


def row_spots(ntno, naux, size, parity=None):
    share, part = ntno // naux, size // naux
    a = lax.broadcasted_iota(jnp.int32, (ntno, size), 0)
    there = lax.broadcasted_iota(jnp.int32, (ntno, size), 1)
    member, place = a // share, a % share
    if parity is None:
        hit = member * part + place == there
    else:
        hit = (member * part + share + place // 2 == there) & (place % 2 == parity)
    return hit.astype(F32).astype(BF)


def spread(ntno, naux, own, last, pieces, out_ref):
    size, width = out_ref.shape
    share, part = ntno // naux, size // naux
    tiles = 0 if pieces is None else pieces.shape[0] // size
    first = width - 5 * LANES
    for parity in range(2):
        add = mm_tn(row_spots(ntno, naux, size, parity), last)
        low = first + 2 * parity * LANES
        out_ref[:, low : low + 2 * LANES] = (own[:, low : low + 2 * LANES] + add).astype(BF)
    for x in range(tiles):
        low = x * LANES
        piece = pieces[x * size : (x + 1) * size]
        out_ref[:, low : low + LANES] = (own[:, low : low + LANES] + piece).astype(BF)
    if tiles == 0:
        out_ref[:, :first] = own[:, :first].astype(BF)
    out_ref[:, first + 4 * LANES :] = own[:, first + 4 * LANES :].astype(BF)


def gather_last(ntno, naux, came):
    size, width = came.shape
    first = width - 5 * LANES
    return sum(
        mm(
            row_spots(ntno, naux, size, parity),
            came[:, first + 2 * parity * LANES : first + 2 * (parity + 1) * LANES],
        )
        for parity in range(2)
    )


def gather_pieces(came):
    tiles = came.shape[1] // LANES - 5
    return jnp.concatenate([came[:, x * LANES : (x + 1) * LANES] for x in range(tiles)], axis=0)


def old_kernel(naux, old_ref, out_ref):
    share, nsq = old_ref.shape[1:]
    slab = nsq // naux
    size, width = out_ref.shape
    part = size // naux
    own, last = [], []
    for member in range(naux):
        row = jnp.concatenate([old_ref[member], jnp.zeros((share, width - nsq), F32)], axis=1)
        own.append(jnp.concatenate([row, jnp.zeros((part - share, width), F32)], axis=0))
        last.append(
            jnp.concatenate(
                [
                    old_ref[naux][:, member * slab : (member + 1) * slab],
                    jnp.zeros((share, 2 * LANES - slab), F32),
                ],
                axis=1,
            )
        )
    own, last = jnp.concatenate(own, axis=0), jnp.concatenate(last, axis=0).astype(BF)
    spread(share * naux, naux, own, last, None, out_ref)


def pack_kernel(route_ref, arrived_ref, old_ref, out_ref):
    size = out_ref.shape[0]
    handed = mm(route_ref[...], arrived_ref[...])
    tiles = handed.shape[0] // size
    for x in range(tiles):
        low = x * LANES
        piece = handed[x * size : (x + 1) * size] + old_ref[:, low : low + LANES].astype(F32)
        out_ref[:, low : low + LANES] = piece.astype(BF)
    out_ref[:, tiles * LANES :] = old_ref[:, tiles * LANES :]


def block_mask(rows, row_block, cols, col_block):
    row = lax.broadcasted_iota(jnp.int32, (rows, cols), 0) // row_block
    return row == lax.broadcasted_iota(jnp.int32, (rows, cols), 1) // col_block


def fetch_order(naux, chunk, wide=None):
    size = naux * 6 * chunk
    here = jnp.arange(size)
    k, source, piece = here // (naux * chunk), (here // chunk) % naux, here % chunk
    at = k * chunk + piece
    if wide is None:
        spot = source * 6 * chunk + at
    else:
        share, part, tiles = wide
        size = tiles * naux * part
        spot = (at % tiles) * (naux * part) + source * part + share + at // tiles
    return (spot[:, None] == jnp.arange(size)[None, :]).astype(BF)


def project(naux, chunk, ordered, covers, pieces):
    npno, width = covers.shape[1], covers.shape[0]
    half_rows = naux * chunk
    stack = []
    for k in range(3):
        block = ordered[k * half_rows : (k + 1) * half_rows]
        stack += [block[:, :npno], block[:, npno:]]
    stack = jnp.concatenate(stack, axis=0).astype(BF)
    mask = block_mask(3 * npno, npno, width, width // 3)
    half = jnp.where(mask, mm_nt(stack, covers), 0.0).astype(BF)
    return mm_tn(pieces, half).astype(BF)


def residual(naux, chunk, new, covers, pieces, matrix):
    npno, width = covers.shape[1], covers.shape[0]
    half_rows = naux * chunk
    mask = block_mask(3 * npno, npno, width, width // 3)
    high, low = high_low(mm_nt(new, matrix))
    left = jnp.where(mask, mm(pieces, high) + mm(pieces, low), 0.0)
    high, low = high_low(left)
    back = mm(high, covers) + mm(low, covers)
    packed = []
    for k in range(3):
        block = back[2 * k * half_rows : 2 * (k + 1) * half_rows]
        packed.append(jnp.concatenate([block[:half_rows], block[half_rows:]], axis=1))
    return jnp.concatenate(packed, axis=0)


def project_both(naux, chunk, order, came, cover_ref, piece_ref):
    ordered = mm(order, came)
    rows = ordered.shape[0] // 2
    return [
        project(
            naux, chunk, ordered[w * rows : (w + 1) * rows], cover_ref[w], piece_ref[w]
        )
        for w in range(2)
    ]


def work_both(naux, chunk, projs, cover_ref, piece_ref, col_ref, row_ref, states, mats):
    wide = mats[0].shape[1]
    start = up(wide, LANES)
    spans = ((0, wide), (start, start + mats[1].shape[1]))
    new, sent = [], []
    for w in range(2):
        den = col_ref[w] + row_ref[:, spans[w][0] : spans[w][1]]
        new.append((SHIFT_LEVEL * states[w] + mm(projs[w], mats[w])) / den)
    halves = [x.astype(BF) for x in new]
    for w in range(2):
        sent.append(residual(naux, chunk, halves[w], cover_ref[w], piece_ref[w], mats[w]))
    return new, halves, jnp.concatenate(sent, axis=0).astype(BF)


def relayout_kernel(ntno, share, rows_ref, own_ref, last_ref, wide_ref):
    nsq = ntno * ntno
    wide_ref[...] = rows_ref[...].astype(F32)
    own = [wide_ref[pl.ds(b, ntno, stride=ntno), :] for b in range(ntno)]
    last = [wide_ref[pl.ds(nsq + b * ntno, ntno), :] for b in range(share)]
    for parts, out in ((own, own_ref), (last, last_ref)):
        out[...] = jnp.concatenate(
            [
                jnp.concatenate([x[:, m * ntno : (m + 1) * ntno] for x in parts], axis=1)
                for m in range(3)
            ],
            axis=0,
        ).astype(BF)


def first_kernel(
    naux,
    chunk,
    came_ref,
    order_ref,
    later_order_ref,
    cover_ref,
    piece_ref,
    col_ref,
    row_ref,
    own_mat_ref,
    last_mat_ref,
    sent_ref,
    own_ref,
    last_ref,
):
    ntno, nsq = own_ref.shape
    slab = last_ref.shape[1]
    came = came_ref[...]
    pieces = gather_pieces(came)
    projs = project_both(naux, chunk, order_ref[...], pieces, cover_ref, piece_ref)
    old = mm(row_spots(ntno, naux, came.shape[0]), came)
    old_last = gather_last(ntno, naux, came)
    new, _, sent = work_both(
        naux,
        chunk,
        projs,
        cover_ref,
        piece_ref,
        col_ref,
        row_ref,
        (old[:, :nsq], old_last[:, :slab]),
        (own_mat_ref[...], last_mat_ref[...]),
    )
    own_ref[...] = new[0]
    last_ref[...] = new[1]
    sent_ref[...] = mm_tn(later_order_ref[...], sent).astype(BF)


def later_kernel(
    naux,
    chunk,
    came_ref,
    order_ref,
    last_order_ref,
    cover_ref,
    piece_ref,
    col_ref,
    row_ref,
    own_ref,
    last_ref,
    own_mat_ref,
    last_mat_ref,
    out_ref,
    wide_ref,
    edge_ref,
):
    ntno, nsq = own_ref.shape
    slab = last_ref.shape[1]
    projs = project_both(naux, chunk, order_ref[...], came_ref[...], cover_ref, piece_ref)
    _, halves, sent = work_both(
        naux,
        chunk,
        projs,
        cover_ref,
        piece_ref,
        col_ref,
        row_ref,
        (own_ref[...], last_ref[...]),
        (own_mat_ref[...], last_mat_ref[...]),
    )
    wide_ref[...] = jnp.zeros(wide_ref.shape, BF)
    wide_ref[:, :nsq] = halves[0]
    edge_ref[...] = jnp.zeros(edge_ref.shape, BF)
    edge_ref[:, :slab] = halves[1]
    own = mm_tn(row_spots(ntno, naux, out_ref.shape[0]), wide_ref[...])
    pieces = mm_tn(last_order_ref[...], sent)
    spread(ntno, naux, own, edge_ref[...], pieces, out_ref)


def finish_kernel(naux, came_ref, route_ref, out_ref, sent_ref):
    share, nsq = out_ref.shape[1:]
    ntno, slab = share * naux, nsq // naux
    part = came_ref.shape[0] // naux
    came = came_ref[...]
    sent_ref[...] = mm(route_ref[...], gather_pieces(came)).astype(BF)
    edge = gather_last(ntno, naux, came)
    came = came.astype(F32)
    last = []
    for member in range(naux):
        out_ref[member] = came[member * part : member * part + share, :nsq]
        last.append(edge[member * share : (member + 1) * share, :slab])
    out_ref[naux] = jnp.concatenate(last, axis=1)


def body(
    aux_blocks,
    occ_blocks,
    intersections,
    tno_energy,
    occ_energy,
    tno_rank,
    triples_old,
    pair_amps,
    pno_energy,
    pair_occ,
    pair_rank,
    request_owner,
    request_row,
):
    tdev = aux_blocks.shape[0]
    ntno = tno_energy.shape[1]
    npno = pno_energy.shape[1]
    pdev = pair_amps.shape[0]
    naux = lax.axis_size("aux")
    ntrip = lax.axis_size("trip")
    member = lax.axis_index("aux")
    share = ntno // naux
    nreq = 3 * tdev
    nsq = ntno * ntno
    slab = share * ntno
    start = up(nsq, LANES)
    span = start + up(slab, LANES)
    prow = npno // naux
    chunk = prow * npno // LANES
    slots = ntrip * chunk
    owner = request_owner.reshape(nreq)

    blocks, asking = integral_blocks(
        aux_blocks, occ_blocks, request_owner, request_row, naux, ntrip, chunk
    )
    rows = lax.psum_scatter(blocks, "aux", scatter_dimension=0, tiled=True)[0]
    serve = swap(asking, "trip").reshape(slots, LANES)

    def routing(dest, at):
        k, part = at // chunk, at % chunk
        request = jnp.where(k < 3, 3 * dest + k, 3 * naux + k - 3)
        asked = jnp.sum(
            jnp.where(request[:, None] == jnp.arange(nreq)[None, :], owner[None, :], 0), axis=1
        )
        return ((asked * chunk + part)[:, None] == jnp.arange(slots)[None, :]).astype(BF)

    number = jnp.arange(naux * 6 * chunk)
    route = routing(number // (6 * chunk), number % (6 * chunk))
    part = 8
    tiles = 6 * chunk // (part - share)
    size, width = naux * part, start
    number = jnp.arange(tiles * size)
    place = number % part
    route_first = routing(
        (number % size) // part, jnp.maximum(place - share, 0) * tiles + number // size
    )
    route_first = jnp.where((place >= share)[:, None], route_first, jnp.zeros((), BF))
    packed_old = call(
        functools.partial(old_kernel, naux), jax.ShapeDtypeStruct((size, width), BF)
    )(triples_old)
    route_back, route_last = route.T, route_first.T
    order = fetch_order(naux, chunk)
    order_first = fetch_order(naux, chunk, (share, part, tiles))

    live = jnp.arange(npno)[None, :] < pair_rank[:, None]
    live_p = lax.dynamic_slice_in_dim(live, member * prow, prow, 1)
    energy_p = lax.dynamic_slice_in_dim(pno_energy, member * prow, prow, 1)
    pair_keep = (live_p[:, :, None] & live[:, None, :]).reshape(pdev * chunk, LANES)
    pair_den = (
        energy_p[:, :, None] + pno_energy[:, None, :] + pair_occ[:, None, None] + SHIFT_LEVEL
    ).reshape(pdev * chunk, LANES)
    amps = (
        lax.dynamic_slice_in_dim(pair_amps, member * prow * npno, prow * npno, 1)
        .reshape(pdev * chunk, LANES)
        .astype(F32)
    )
    gain = jnp.zeros_like(amps)

    def two(x):
        return jnp.stack([lax.dynamic_slice_in_dim(x, member, 1, 0)[0], x[naux]])

    masked = jnp.where(jnp.arange(ntno)[None, :] < tno_rank[:, None], tno_energy, jnp.inf)
    energy = two(masked)
    col = two(masked - jnp.sum(occ_energy, axis=1)[:, None] + SHIFT_LEVEL)[:, :, None]
    energy_b = lax.dynamic_slice_in_dim(energy[1], member * share, share, 0)
    row = jnp.concatenate(
        [
            (energy[0][:, None] + energy[0][None, :]).reshape(nsq),
            jnp.zeros((start - nsq,), F32),
            (energy_b[:, None] + energy[1][None, :]).reshape(slab),
            jnp.zeros((span - start - slab,), F32),
        ]
    )[None, :]
    cover = two(intersections)
    flat = cover.transpose(0, 1, 3, 2).reshape(2, 3 * ntno, npno)
    split = cover.reshape(2, 3, npno // 2, 2, ntno).transpose(0, 1, 3, 2, 4)
    split = split.reshape(2, 3 * npno, ntno)

    ready = (
        (serve, route, route_first, route_back, route_last, order, order_first)
        + (pair_keep, pair_den, amps, flat, split, col, row, packed_old)
    )
    serve, route, route_first, route_back, route_last, order, order_first, *ready = (
        lax.optimization_barrier(ready)
    )
    pair_keep, pair_den, amps, flat, split, col, row, packed_old = ready
    for step in range(PASSES):
        outgoing = jnp.where(pair_keep, amps.astype(BF), jnp.zeros((), BF))
        pad = serve.shape[1] - outgoing.shape[0]
        found = mm(serve, jnp.pad(outgoing, ((0, pad), (0, 0)))).astype(BF)
        arrived = swap(found.reshape(ntrip, chunk, LANES), "trip").reshape(slots, LANES)
        if step == 0:
            packed = call(pack_kernel, jax.ShapeDtypeStruct((size, width), BF))(
                route_first, arrived, packed_old
            )
            came = swap(packed.reshape(naux, part, width), "aux")
        else:
            handed = mm(route, arrived).astype(BF).reshape(naux, 6 * chunk, LANES)
            came = swap(handed, "aux")
        if step == 0:
            own_mat, last_mat = call(
                functools.partial(relayout_kernel, ntno, share),
                (
                    jax.ShapeDtypeStruct((3 * ntno, nsq), BF),
                    jax.ShapeDtypeStruct((3 * ntno, slab), BF),
                ),
                [pltpu.VMEM(rows.shape, F32)],
            )(rows)
            sent, own, last = call(
                functools.partial(first_kernel, naux, chunk),
                (
                    jax.ShapeDtypeStruct((naux * 6 * chunk, LANES), BF),
                    jax.ShapeDtypeStruct((ntno, nsq), F32),
                    jax.ShapeDtypeStruct((ntno, slab), F32),
                ),
            )(
                came.reshape(-1, width),
                order_first,
                order,
                flat,
                split,
                col,
                row,
                own_mat,
                last_mat,
            )
            came = swap(sent.reshape(naux, 6 * chunk, LANES), "aux")
            sent = mm(route_back, came.reshape(naux * 6 * chunk, LANES))
        else:
            sent = call(
                functools.partial(later_kernel, naux, chunk),
                jax.ShapeDtypeStruct((size, width), BF),
                [pltpu.VMEM((ntno, width), BF), pltpu.VMEM((ntno, 2 * LANES), BF)],
            )(
                came.reshape(-1, LANES),
                order,
                order_first,
                flat,
                split,
                col,
                row,
                own,
                last,
                own_mat,
                last_mat,
            )
            came = swap(sent.reshape(naux, part, width), "aux").reshape(size, width)
            triples_new, sent = call(
                functools.partial(finish_kernel, naux),
                (
                    jax.ShapeDtypeStruct((tdev, share, nsq), F32),
                    jax.ShapeDtypeStruct((slots, LANES), BF),
                ),
            )(came, route_last)
        sent = sent.astype(BF).reshape(ntrip, chunk, LANES)
        came = swap(sent, "trip").reshape(slots, LANES)
        total = mm_tn(serve, came)[: pdev * chunk]
        change = jnp.where(pair_keep, total / pair_den, 0.0)
        gain = gain + change
        amps = amps + change

    gains = jnp.broadcast_to(gain.astype(BF)[None], (naux, pdev * chunk, LANES))
    gains = swap(gains, "aux").reshape(naux, pdev, prow * npno).transpose(1, 0, 2)
    pairs_new = pair_amps.astype(F32) + gains.reshape(pdev, npno * npno).astype(F32)
    return triples_new, pairs_new


def solution(mesh):
    in_specs = (
        P("trip", "aux", None),
        P("trip", "aux", None),
        P("trip", None, None, None),
        P("trip", None),
        P("trip", None),
        P("trip"),
        P("trip", "aux", None),
        P("trip", None),
        P("trip", None),
        P("trip"),
        P("trip"),
        P("trip", None, None),
        P("trip", None),
    )
    out_specs = (P("trip", "aux", None), P("trip", None))
    return jax.shard_map(body, mesh=mesh, in_specs=in_specs, out_specs=out_specs, check_vma=False)
```

```python
import functools
import jax
import jax.numpy as jnp
from jax import lax
from jax.experimental import pallas as pl
from jax.experimental.pallas import tpu as pltpu
from jax.sharding import PartitionSpec as P

PASSES = 2
SHIFT_LEVEL = 1.0
BF = jnp.bfloat16
F32 = jnp.float32
LANES = 128
VMEM_LIMIT = 48 * 2**20
VMEM_ALL = 63 * 2**20


def mm(x, y):
    return jnp.dot(x, y, preferred_element_type=F32)


def mm_nt(x, y):
    return lax.dot_general(x, y, (((1,), (1,)), ((), ())), preferred_element_type=F32)


def mm_tn(x, y):
    return lax.dot_general(x, y, (((0,), (0,)), ((), ())), preferred_element_type=F32)


def high_low(x):
    high = x.astype(BF)
    return high, (x - high.astype(F32)).astype(BF)


def swap(x, axis):
    return lax.all_to_all(x, axis, split_axis=0, concat_axis=0, tiled=True)


def up(n, m):
    return -(-n // m) * m


def call(kernel, outs, scratch=(), limit=VMEM_LIMIT, **specs):
    return pl.pallas_call(
        kernel,
        out_shape=outs,
        scratch_shapes=list(scratch),
        **specs,
        compiler_params=pltpu.CompilerParams(vmem_limit_bytes=limit),
    )


def blocks_kernel(
    naux,
    share,
    aux_ref,
    occ_far_ref,
    owner_far_ref,
    local_far_ref,
    out_ref,
    asking_out_ref,
    held_ref,
    made_ref,
    last_ref,
    occ_ref,
    owner_ref,
    local_ref,
    asking_ref,
    in_sems,
    out_sems,
    more_sems,
):
    nsq, depth = held_ref.shape[1:]
    width = occ_ref.shape[1]
    ntno = share * naux
    groups = [naux // 2, 0]
    ends = [naux + 1, naux // 2]
    arriving = []
    for n, (t, end) in enumerate(zip(groups, ends)):
        part = pl.ds(t, end - t)
        copy = pltpu.make_async_copy(aux_ref.at[part], held_ref.at[part], in_sems.at[n])
        copy.start()
        arriving.append(copy)
    pairs = ((owner_far_ref, owner_ref), (local_far_ref, local_ref), (occ_far_ref, occ_ref))
    first = [pltpu.make_async_copy(x, y, more_sems.at[n]) for n, (x, y) in enumerate(pairs)]
    for copy in first:
        copy.start()
    for copy in first:
        copy.wait()
    chunk = asking_ref.shape[1]
    asking_ref[...] = jnp.zeros(asking_ref.shape, BF)
    piece = lax.broadcasted_iota(jnp.int32, (chunk, LANES), 0)
    lane = lax.broadcasted_iota(jnp.int32, (chunk, LANES), 1)
    for m in range(local_ref.shape[0]):
        for t in range(local_ref.shape[1]):
            hot = (lane == local_ref[m, t] * chunk + piece).astype(F32).astype(BF)
            asking_ref[pl.ds(owner_ref[m, 0, t], 1)] = hot[None]
    asked = pltpu.make_async_copy(asking_ref, asking_out_ref, more_sems.at[3])
    asked.start()

    none = jnp.zeros((LANES - width, depth), BF)
    zero = jnp.zeros((LANES, depth), BF)
    rest = made_ref.shape[1] - nsq - share * ntno
    leaving = []
    for n, (low, end) in enumerate(zip(groups, ends)):
        arriving[n].wait()
        if end > naux:
            right = jnp.concatenate([occ_ref[naux], none], axis=0)
            last_ref[:nsq, :] = mm_nt(held_ref[naux], right)
        top = min(end, naux)
        for t in range(low, top, 2):
            left = jnp.concatenate([held_ref[t], held_ref[t + 1]], axis=1)
            upper = jnp.concatenate([occ_ref[t], none, zero], axis=0)
            lower = jnp.concatenate([zero, occ_ref[t + 1], none], axis=0)
            both = mm_nt(left, jnp.concatenate([upper, lower], axis=1)).astype(BF)
            made_ref[t, :nsq, :] = both[:, :LANES]
            made_ref[t + 1, :nsq, :] = both[:, LANES:]
            for member in (t, t + 1):
                parts = [
                    last_ref[pl.ds(member * share + b, ntno, stride=ntno), :]
                    for b in range(share)
                ]
                parts.append(jnp.zeros((rest, LANES), F32))
                made_ref[member, nsq:, :] = jnp.concatenate(parts, axis=0).astype(BF)
        part = pl.ds(low, top - low)
        copy = pltpu.make_async_copy(made_ref.at[part], out_ref.at[part], out_sems.at[n])
        copy.start()
        leaving.append(copy)
    for copy in leaving:
        copy.wait()
    asked.wait()


def integral_blocks(aux_blocks, occ_blocks, request_owner, request_row, naux, ntrip, chunk):
    tdev, depth, nsq = aux_blocks.shape
    ntno = occ_blocks.shape[2] // 3
    share = ntno // naux
    rows = up(nsq + share * ntno, 16)
    far = pl.BlockSpec(memory_space=pltpu.HBM)
    return call(
        functools.partial(blocks_kernel, naux, share),
        (
            jax.ShapeDtypeStruct((naux, rows, LANES), BF),
            jax.ShapeDtypeStruct((ntrip, chunk, LANES), BF),
        ),
        [
            pltpu.VMEM((tdev, nsq, depth), BF),
            pltpu.VMEM((naux, rows, LANES), BF),
            pltpu.VMEM((nsq + ntno, LANES), F32),
            pltpu.VMEM((tdev, occ_blocks.shape[2], depth), BF),
            pltpu.SMEM((3, 1, tdev), jnp.int32),
            pltpu.SMEM((3, tdev), jnp.int32),
            pltpu.VMEM((ntrip, chunk, LANES), BF),
            pltpu.SemaphoreType.DMA((2,)),
            pltpu.SemaphoreType.DMA((2,)),
            pltpu.SemaphoreType.DMA((4,)),
        ],
        VMEM_ALL,
        in_specs=[far] * 4,
        out_specs=(far, far),
    )(
        aux_blocks.transpose(0, 2, 1),
        occ_blocks.transpose(0, 2, 1),
        request_owner.transpose(1, 2, 0),
        request_row.T,
    )


def row_spots(ntno, naux, size, parity=None):
    share, part = ntno // naux, size // naux
    a = lax.broadcasted_iota(jnp.int32, (ntno, size), 0)
    there = lax.broadcasted_iota(jnp.int32, (ntno, size), 1)
    member, place = a // share, a % share
    if parity is None:
        hit = member * part + place == there
    else:
        hit = (member * part + share + place // 2 == there) & (place % 2 == parity)
    return hit.astype(F32).astype(BF)


def spread(ntno, naux, own, last, pieces, out_ref):
    size, width = out_ref.shape
    share, part = ntno // naux, size // naux
    tiles = 0 if pieces is None else pieces.shape[0] // size
    first = width - 5 * LANES
    for parity in range(2):
        add = mm_tn(row_spots(ntno, naux, size, parity), last)
        low = first + 2 * parity * LANES
        out_ref[:, low : low + 2 * LANES] = (own[:, low : low + 2 * LANES] + add).astype(BF)
    for x in range(tiles):
        low = x * LANES
        piece = pieces[x * size : (x + 1) * size]
        out_ref[:, low : low + LANES] = (own[:, low : low + LANES] + piece).astype(BF)
    if tiles == 0:
        out_ref[:, :first] = own[:, :first].astype(BF)
    out_ref[:, first + 4 * LANES :] = own[:, first + 4 * LANES :].astype(BF)


def gather_last(ntno, naux, came):
    size, width = came.shape
    first = width - 5 * LANES
    return sum(
        mm(
            row_spots(ntno, naux, size, parity),
            came[:, first + 2 * parity * LANES : first + 2 * (parity + 1) * LANES],
        )
        for parity in range(2)
    )


def gather_pieces(came):
    tiles = came.shape[1] // LANES - 5
    return jnp.concatenate([came[:, x * LANES : (x + 1) * LANES] for x in range(tiles)], axis=0)


def old_kernel(naux, old_ref, out_ref):
    share, nsq = old_ref.shape[1:]
    slab = nsq // naux
    size, width = out_ref.shape
    part = size // naux
    own, last = [], []
    for member in range(naux):
        row = jnp.concatenate([old_ref[member], jnp.zeros((share, width - nsq), F32)], axis=1)
        own.append(jnp.concatenate([row, jnp.zeros((part - share, width), F32)], axis=0))
        last.append(
            jnp.concatenate(
                [
                    old_ref[naux][:, member * slab : (member + 1) * slab],
                    jnp.zeros((share, 2 * LANES - slab), F32),
                ],
                axis=1,
            )
        )
    own, last = jnp.concatenate(own, axis=0), jnp.concatenate(last, axis=0).astype(BF)
    spread(share * naux, naux, own, last, None, out_ref)


def pack_kernel(route_ref, arrived_ref, old_ref, out_ref):
    size = out_ref.shape[0]
    handed = mm(route_ref[...], arrived_ref[...])
    tiles = handed.shape[0] // size
    for x in range(tiles):
        low = x * LANES
        piece = handed[x * size : (x + 1) * size] + old_ref[:, low : low + LANES].astype(F32)
        out_ref[:, low : low + LANES] = piece.astype(BF)
    out_ref[:, tiles * LANES :] = old_ref[:, tiles * LANES :]


def block_mask(rows, row_block, cols, col_block):
    row = lax.broadcasted_iota(jnp.int32, (rows, cols), 0) // row_block
    return row == lax.broadcasted_iota(jnp.int32, (rows, cols), 1) // col_block


def fetch_order(naux, chunk, wide=None):
    size = naux * 6 * chunk
    here = jnp.arange(size)
    k, source, piece = here // (naux * chunk), (here // chunk) % naux, here % chunk
    at = k * chunk + piece
    if wide is None:
        spot = source * 6 * chunk + at
    else:
        share, part, tiles = wide
        size = tiles * naux * part
        spot = (at % tiles) * (naux * part) + source * part + share + at // tiles
    return (spot[:, None] == jnp.arange(size)[None, :]).astype(BF)


def project(naux, chunk, ordered, covers, pieces):
    npno, width = covers.shape[1], covers.shape[0]
    half_rows = naux * chunk
    stack = []
    for k in range(3):
        block = ordered[k * half_rows : (k + 1) * half_rows]
        stack += [block[:, :npno], block[:, npno:]]
    stack = jnp.concatenate(stack, axis=0).astype(BF)
    mask = block_mask(3 * npno, npno, width, width // 3)
    half = jnp.where(mask, mm_nt(stack, covers), 0.0).astype(BF)
    return mm_tn(pieces, half).astype(BF)


def residual(naux, chunk, new, covers, pieces, matrix):
    npno, width = covers.shape[1], covers.shape[0]
    half_rows = naux * chunk
    mask = block_mask(3 * npno, npno, width, width // 3)
    high, low = high_low(mm_nt(new, matrix))
    left = jnp.where(mask, mm(pieces, high) + mm(pieces, low), 0.0)
    high, low = high_low(left)
    back = mm(high, covers) + mm(low, covers)
    packed = []
    for k in range(3):
        block = back[2 * k * half_rows : 2 * (k + 1) * half_rows]
        packed.append(jnp.concatenate([block[:half_rows], block[half_rows:]], axis=1))
    return jnp.concatenate(packed, axis=0)


def project_both(naux, chunk, order, came, cover_ref, piece_ref):
    ordered = mm(order, came)
    rows = ordered.shape[0] // 2
    return [
        project(
            naux, chunk, ordered[w * rows : (w + 1) * rows], cover_ref[w], piece_ref[w]
        )
        for w in range(2)
    ]


def work_both(naux, chunk, projs, cover_ref, piece_ref, col_ref, row_ref, states, mats):
    wide = mats[0].shape[1]
    start = up(wide, LANES)
    spans = ((0, wide), (start, start + mats[1].shape[1]))
    new, sent = [], []
    for w in range(2):
        den = col_ref[w] + row_ref[:, spans[w][0] : spans[w][1]]
        new.append((SHIFT_LEVEL * states[w] + mm(projs[w], mats[w])) / den)
    halves = [x.astype(BF) for x in new]
    for w in range(2):
        sent.append(residual(naux, chunk, halves[w], cover_ref[w], piece_ref[w], mats[w]))
    return new, halves, jnp.concatenate(sent, axis=0).astype(BF)


def relayout_kernel(ntno, share, rows_ref, own_ref, last_ref, wide_ref):
    nsq = ntno * ntno
    wide_ref[...] = rows_ref[...].astype(F32)
    own = [wide_ref[pl.ds(b, ntno, stride=ntno), :] for b in range(ntno)]
    last = [wide_ref[pl.ds(nsq + b * ntno, ntno), :] for b in range(share)]
    for parts, out in ((own, own_ref), (last, last_ref)):
        out[...] = jnp.concatenate(
            [
                jnp.concatenate([x[:, m * ntno : (m + 1) * ntno] for x in parts], axis=1)
                for m in range(3)
            ],
            axis=0,
        ).astype(BF)


def first_kernel(
    naux,
    chunk,
    came_ref,
    order_ref,
    later_order_ref,
    cover_ref,
    piece_ref,
    col_ref,
    row_ref,
    own_mat_ref,
    last_mat_ref,
    sent_ref,
    own_ref,
    last_ref,
):
    ntno, nsq = own_ref.shape
    slab = last_ref.shape[1]
    came = came_ref[...]
    pieces = gather_pieces(came)
    projs = project_both(naux, chunk, order_ref[...], pieces, cover_ref, piece_ref)
    old = mm(row_spots(ntno, naux, came.shape[0]), came)
    old_last = gather_last(ntno, naux, came)
    new, _, sent = work_both(
        naux,
        chunk,
        projs,
        cover_ref,
        piece_ref,
        col_ref,
        row_ref,
        (old[:, :nsq], old_last[:, :slab]),
        (own_mat_ref[...], last_mat_ref[...]),
    )
    own_ref[...] = new[0]
    last_ref[...] = new[1]
    sent_ref[...] = mm_tn(later_order_ref[...], sent).astype(BF)


def later_kernel(
    naux,
    chunk,
    came_ref,
    order_ref,
    last_order_ref,
    cover_ref,
    piece_ref,
    col_ref,
    row_ref,
    own_ref,
    last_ref,
    own_mat_ref,
    last_mat_ref,
    out_ref,
    wide_ref,
    edge_ref,
):
    ntno, nsq = own_ref.shape
    slab = last_ref.shape[1]
    projs = project_both(naux, chunk, order_ref[...], came_ref[...], cover_ref, piece_ref)
    _, halves, sent = work_both(
        naux,
        chunk,
        projs,
        cover_ref,
        piece_ref,
        col_ref,
        row_ref,
        (own_ref[...], last_ref[...]),
        (own_mat_ref[...], last_mat_ref[...]),
    )
    wide_ref[...] = jnp.zeros(wide_ref.shape, BF)
    wide_ref[:, :nsq] = halves[0]
    edge_ref[...] = jnp.zeros(edge_ref.shape, BF)
    edge_ref[:, :slab] = halves[1]
    own = mm_tn(row_spots(ntno, naux, out_ref.shape[0]), wide_ref[...])
    pieces = mm_tn(last_order_ref[...], sent)
    spread(ntno, naux, own, edge_ref[...], pieces, out_ref)


def finish_kernel(naux, came_ref, route_ref, out_ref, sent_ref):
    share, nsq = out_ref.shape[1:]
    ntno, slab = share * naux, nsq // naux
    part = came_ref.shape[0] // naux
    came = came_ref[...]
    sent_ref[...] = mm(route_ref[...], gather_pieces(came)).astype(BF)
    edge = gather_last(ntno, naux, came)
    came = came.astype(F32)
    last = []
    for member in range(naux):
        out_ref[member] = came[member * part : member * part + share, :nsq]
        last.append(edge[member * share : (member + 1) * share, :slab])
    out_ref[naux] = jnp.concatenate(last, axis=1)


def body(
    aux_blocks,
    occ_blocks,
    intersections,
    tno_energy,
    occ_energy,
    tno_rank,
    triples_old,
    pair_amps,
    pno_energy,
    pair_occ,
    pair_rank,
    request_owner,
    request_row,
):
    tdev = aux_blocks.shape[0]
    ntno = tno_energy.shape[1]
    npno = pno_energy.shape[1]
    pdev = pair_amps.shape[0]
    naux = lax.axis_size("aux")
    ntrip = lax.axis_size("trip")
    member = lax.axis_index("aux")
    share = ntno // naux
    nreq = 3 * tdev
    nsq = ntno * ntno
    slab = share * ntno
    start = up(nsq, LANES)
    span = start + up(slab, LANES)
    prow = npno // naux
    chunk = prow * npno // LANES
    slots = ntrip * chunk
    owner = request_owner.reshape(nreq)

    blocks, asking = integral_blocks(
        aux_blocks, occ_blocks, request_owner, request_row, naux, ntrip, chunk
    )
    rows = lax.psum_scatter(blocks, "aux", scatter_dimension=0, tiled=True)[0]
    serve = swap(asking, "trip").reshape(slots, LANES)

    def routing(dest, at):
        k, part = at // chunk, at % chunk
        request = jnp.where(k < 3, 3 * dest + k, 3 * naux + k - 3)
        asked = jnp.sum(
            jnp.where(request[:, None] == jnp.arange(nreq)[None, :], owner[None, :], 0), axis=1
        )
        return ((asked * chunk + part)[:, None] == jnp.arange(slots)[None, :]).astype(BF)

    number = jnp.arange(naux * 6 * chunk)
    route = routing(number // (6 * chunk), number % (6 * chunk))
    part = 8
    tiles = 6 * chunk // (part - share)
    size, width = naux * part, start
    number = jnp.arange(tiles * size)
    place = number % part
    route_first = routing(
        (number % size) // part, jnp.maximum(place - share, 0) * tiles + number // size
    )
    route_first = jnp.where((place >= share)[:, None], route_first, jnp.zeros((), BF))
    packed_old = call(
        functools.partial(old_kernel, naux), jax.ShapeDtypeStruct((size, width), BF)
    )(triples_old)
    route_back, route_last = route.T, route_first.T
    order = fetch_order(naux, chunk)
    order_first = fetch_order(naux, chunk, (share, part, tiles))

    live = jnp.arange(npno)[None, :] < pair_rank[:, None]
    live_p = lax.dynamic_slice_in_dim(live, member * prow, prow, 1)
    energy_p = lax.dynamic_slice_in_dim(pno_energy, member * prow, prow, 1)
    pair_keep = (live_p[:, :, None] & live[:, None, :]).reshape(pdev * chunk, LANES)
    pair_den = (
        energy_p[:, :, None] + pno_energy[:, None, :] + pair_occ[:, None, None] + SHIFT_LEVEL
    ).reshape(pdev * chunk, LANES)
    amps = (
        lax.dynamic_slice_in_dim(pair_amps, member * prow * npno, prow * npno, 1)
        .reshape(pdev * chunk, LANES)
        .astype(F32)
    )
    gain = jnp.zeros_like(amps)

    def two(x):
        return jnp.stack([lax.dynamic_slice_in_dim(x, member, 1, 0)[0], x[naux]])

    masked = jnp.where(jnp.arange(ntno)[None, :] < tno_rank[:, None], tno_energy, jnp.inf)
    energy = two(masked)
    col = two(masked - jnp.sum(occ_energy, axis=1)[:, None] + SHIFT_LEVEL)[:, :, None]
    energy_b = lax.dynamic_slice_in_dim(energy[1], member * share, share, 0)
    row = jnp.concatenate(
        [
            (energy[0][:, None] + energy[0][None, :]).reshape(nsq),
            jnp.zeros((start - nsq,), F32),
            (energy_b[:, None] + energy[1][None, :]).reshape(slab),
            jnp.zeros((span - start - slab,), F32),
        ]
    )[None, :]
    cover = two(intersections)
    flat = cover.transpose(0, 1, 3, 2).reshape(2, 3 * ntno, npno)
    split = cover.reshape(2, 3, npno // 2, 2, ntno).transpose(0, 1, 3, 2, 4)
    split = split.reshape(2, 3 * npno, ntno)

    ready = (
        (serve, route, route_first, route_back, route_last, order, order_first)
        + (pair_keep, pair_den, amps, flat, split, col, row, packed_old)
    )
    serve, route, route_first, route_back, route_last, order, order_first, *ready = (
        lax.optimization_barrier(ready)
    )
    pair_keep, pair_den, amps, flat, split, col, row, packed_old = ready
    for step in range(PASSES):
        outgoing = jnp.where(pair_keep, amps.astype(BF), jnp.zeros((), BF))
        pad = serve.shape[1] - outgoing.shape[0]
        found = mm(serve, jnp.pad(outgoing, ((0, pad), (0, 0)))).astype(BF)
        arrived = swap(found.reshape(ntrip, chunk, LANES), "trip").reshape(slots, LANES)
        if step == 0:
            packed = call(pack_kernel, jax.ShapeDtypeStruct((size, width), BF))(
                route_first, arrived, packed_old
            )
            came = swap(packed.reshape(naux, part, width), "aux")
        else:
            handed = mm(route, arrived).astype(BF).reshape(naux, 6 * chunk, LANES)
            came = swap(handed, "aux")
        if step == 0:
            own_mat, last_mat = call(
                functools.partial(relayout_kernel, ntno, share),
                (
                    jax.ShapeDtypeStruct((3 * ntno, nsq), BF),
                    jax.ShapeDtypeStruct((3 * ntno, slab), BF),
                ),
                [pltpu.VMEM(rows.shape, F32)],
            )(rows)
            sent, own, last = call(
                functools.partial(first_kernel, naux, chunk),
                (
                    jax.ShapeDtypeStruct((naux * 6 * chunk, LANES), BF),
                    jax.ShapeDtypeStruct((ntno, nsq), F32),
                    jax.ShapeDtypeStruct((ntno, slab), F32),
                ),
            )(
                came.reshape(-1, width),
                order_first,
                order,
                flat,
                split,
                col,
                row,
                own_mat,
                last_mat,
            )
            came = swap(sent.reshape(naux, 6 * chunk, LANES), "aux")
            sent = mm(route_back, came.reshape(naux * 6 * chunk, LANES))
        else:
            sent = call(
                functools.partial(later_kernel, naux, chunk),
                jax.ShapeDtypeStruct((size, width), BF),
                [pltpu.VMEM((ntno, width), BF), pltpu.VMEM((ntno, 2 * LANES), BF)],
            )(
                came.reshape(-1, LANES),
                order,
                order_first,
                flat,
                split,
                col,
                row,
                own,
                last,
                own_mat,
                last_mat,
            )
            came = swap(sent.reshape(naux, part, width), "aux").reshape(size, width)
            triples_new, sent = call(
                functools.partial(finish_kernel, naux),
                (
                    jax.ShapeDtypeStruct((tdev, share, nsq), F32),
                    jax.ShapeDtypeStruct((slots, LANES), BF),
                ),
            )(came, route_last)
        sent = sent.astype(BF).reshape(ntrip, chunk, LANES)
        came = swap(sent, "trip").reshape(slots, LANES)
        total = mm_tn(serve, came)[: pdev * chunk]
        change = jnp.where(pair_keep, total / pair_den, 0.0)
        gain = gain + change
        amps = amps + change

    gains = jnp.broadcast_to(gain.astype(BF)[None], (naux, pdev * chunk, LANES))
    gains = swap(gains, "aux").reshape(naux, pdev, prow * npno).transpose(1, 0, 2)
    pairs_new = pair_amps.astype(F32) + gains.reshape(pdev, npno * npno).astype(F32)
    return triples_new, pairs_new


def solution(mesh):
    in_specs = (
        P("trip", "aux", None),
        P("trip", "aux", None),
        P("trip", None, None, None),
        P("trip", None),
        P("trip", None),
        P("trip"),
        P("trip", "aux", None),
        P("trip", None),
        P("trip", None),
        P("trip"),
        P("trip"),
        P("trip", None, None),
        P("trip", None),
    )
    out_specs = (P("trip", "aux", None), P("trip", None))
    return jax.shard_map(body, mesh=mesh, in_specs=in_specs, out_specs=out_specs, check_vma=False)
```

```python
import functools
import jax
import jax.numpy as jnp
from jax import lax
from jax.experimental import pallas as pl
from jax.experimental.pallas import tpu as pltpu
from jax.sharding import PartitionSpec as P

PASSES = 2
SHIFT_LEVEL = 1.0
BF = jnp.bfloat16
F32 = jnp.float32
LANES = 128
VMEM_LIMIT = 48 * 2**20
VMEM_ALL = 63 * 2**20


def mm(x, y):
    return jnp.dot(x, y, preferred_element_type=F32)


def mm_nt(x, y):
    return lax.dot_general(x, y, (((1,), (1,)), ((), ())), preferred_element_type=F32)


def mm_tn(x, y):
    return lax.dot_general(x, y, (((0,), (0,)), ((), ())), preferred_element_type=F32)


def high_low(x):
    high = x.astype(BF)
    return high, (x - high.astype(F32)).astype(BF)


def swap(x, axis):
    return lax.all_to_all(x, axis, split_axis=0, concat_axis=0, tiled=True)


def up(n, m):
    return -(-n // m) * m


def call(kernel, outs, scratch=(), limit=VMEM_LIMIT, **specs):
    return pl.pallas_call(
        kernel,
        out_shape=outs,
        scratch_shapes=list(scratch),
        **specs,
        compiler_params=pltpu.CompilerParams(vmem_limit_bytes=limit),
    )


def blocks_kernel(
    naux,
    share,
    aux_ref,
    occ_far_ref,
    owner_far_ref,
    local_far_ref,
    out_ref,
    asking_out_ref,
    held_ref,
    made_ref,
    last_ref,
    occ_ref,
    owner_ref,
    local_ref,
    asking_ref,
    in_sems,
    out_sems,
    more_sems,
):
    nsq, depth = held_ref.shape[1:]
    width = occ_ref.shape[1]
    ntno = share * naux
    groups = [naux // 2, 0]
    ends = [naux + 1, naux // 2]
    arriving = []
    for n, (t, end) in enumerate(zip(groups, ends)):
        part = pl.ds(t, end - t)
        copy = pltpu.make_async_copy(aux_ref.at[part], held_ref.at[part], in_sems.at[n])
        copy.start()
        arriving.append(copy)
    pairs = ((owner_far_ref, owner_ref), (local_far_ref, local_ref), (occ_far_ref, occ_ref))
    first = [pltpu.make_async_copy(x, y, more_sems.at[n]) for n, (x, y) in enumerate(pairs)]
    for copy in first:
        copy.start()
    for copy in first:
        copy.wait()
    chunk = asking_ref.shape[1]
    asking_ref[...] = jnp.zeros(asking_ref.shape, BF)
    piece = lax.broadcasted_iota(jnp.int32, (chunk, LANES), 0)
    lane = lax.broadcasted_iota(jnp.int32, (chunk, LANES), 1)
    for m in range(local_ref.shape[0]):
        for t in range(local_ref.shape[1]):
            hot = (lane == local_ref[m, t] * chunk + piece).astype(F32).astype(BF)
            asking_ref[pl.ds(owner_ref[m, 0, t], 1)] = hot[None]
    asked = pltpu.make_async_copy(asking_ref, asking_out_ref, more_sems.at[3])
    asked.start()

    none = jnp.zeros((LANES - width, depth), BF)
    zero = jnp.zeros((LANES, depth), BF)
    rest = made_ref.shape[1] - nsq - share * ntno
    leaving = []
    for n, (low, end) in enumerate(zip(groups, ends)):
        arriving[n].wait()
        if end > naux:
            right = jnp.concatenate([occ_ref[naux], none], axis=0)
            last_ref[:nsq, :] = mm_nt(held_ref[naux], right)
        top = min(end, naux)
        for t in range(low, top, 2):
            left = jnp.concatenate([held_ref[t], held_ref[t + 1]], axis=1)
            upper = jnp.concatenate([occ_ref[t], none, zero], axis=0)
            lower = jnp.concatenate([zero, occ_ref[t + 1], none], axis=0)
            both = mm_nt(left, jnp.concatenate([upper, lower], axis=1)).astype(BF)
            made_ref[t, :nsq, :] = both[:, :LANES]
            made_ref[t + 1, :nsq, :] = both[:, LANES:]
            for member in (t, t + 1):
                parts = [
                    last_ref[pl.ds(member * share + b, ntno, stride=ntno), :]
                    for b in range(share)
                ]
                parts.append(jnp.zeros((rest, LANES), F32))
                made_ref[member, nsq:, :] = jnp.concatenate(parts, axis=0).astype(BF)
        part = pl.ds(low, top - low)
        copy = pltpu.make_async_copy(made_ref.at[part], out_ref.at[part], out_sems.at[n])
        copy.start()
        leaving.append(copy)
    for copy in leaving:
        copy.wait()
    asked.wait()


def integral_blocks(aux_blocks, occ_blocks, request_owner, request_row, naux, ntrip, chunk):
    tdev, depth, nsq = aux_blocks.shape
    ntno = occ_blocks.shape[2] // 3
    share = ntno // naux
    rows = up(nsq + share * ntno, 16)
    far = pl.BlockSpec(memory_space=pltpu.HBM)
    return call(
        functools.partial(blocks_kernel, naux, share),
        (
            jax.ShapeDtypeStruct((naux, rows, LANES), BF),
            jax.ShapeDtypeStruct((ntrip, chunk, LANES), BF),
        ),
        [
            pltpu.VMEM((tdev, nsq, depth), BF),
            pltpu.VMEM((naux, rows, LANES), BF),
            pltpu.VMEM((nsq + ntno, LANES), F32),
            pltpu.VMEM((tdev, occ_blocks.shape[2], depth), BF),
            pltpu.SMEM((3, 1, tdev), jnp.int32),
            pltpu.SMEM((3, tdev), jnp.int32),
            pltpu.VMEM((ntrip, chunk, LANES), BF),
            pltpu.SemaphoreType.DMA((2,)),
            pltpu.SemaphoreType.DMA((2,)),
            pltpu.SemaphoreType.DMA((4,)),
        ],
        VMEM_ALL,
        in_specs=[far] * 4,
        out_specs=(far, far),
    )(
        aux_blocks.transpose(0, 2, 1),
        occ_blocks.transpose(0, 2, 1),
        request_owner.transpose(1, 2, 0),
        request_row.T,
    )


def row_spots(ntno, naux, size, parity=None):
    share, part = ntno // naux, size // naux
    a = lax.broadcasted_iota(jnp.int32, (ntno, size), 0)
    there = lax.broadcasted_iota(jnp.int32, (ntno, size), 1)
    member, place = a // share, a % share
    if parity is None:
        hit = member * part + place == there
    else:
        hit = (member * part + share + place // 2 == there) & (place % 2 == parity)
    return hit.astype(F32).astype(BF)


def spread(ntno, naux, own, last, pieces, out_ref):
    size, width = out_ref.shape
    share, part = ntno // naux, size // naux
    tiles = 0 if pieces is None else pieces.shape[0] // size
    first = width - 5 * LANES
    for parity in range(2):
        add = mm_tn(row_spots(ntno, naux, size, parity), last)
        low = first + 2 * parity * LANES
        out_ref[:, low : low + 2 * LANES] = (own[:, low : low + 2 * LANES] + add).astype(BF)
    for x in range(tiles):
        low = x * LANES
        piece = pieces[x * size : (x + 1) * size]
        out_ref[:, low : low + LANES] = (own[:, low : low + LANES] + piece).astype(BF)
    if tiles == 0:
        out_ref[:, :first] = own[:, :first].astype(BF)
    out_ref[:, first + 4 * LANES :] = own[:, first + 4 * LANES :].astype(BF)


def gather_last(ntno, naux, came):
    size, width = came.shape
    first = width - 5 * LANES
    return sum(
        mm(
            row_spots(ntno, naux, size, parity),
            came[:, first + 2 * parity * LANES : first + 2 * (parity + 1) * LANES],
        )
        for parity in range(2)
    )


def gather_pieces(came):
    tiles = came.shape[1] // LANES - 5
    return jnp.concatenate([came[:, x * LANES : (x + 1) * LANES] for x in range(tiles)], axis=0)


def old_kernel(naux, old_ref, out_ref):
    share, nsq = old_ref.shape[1:]
    slab = nsq // naux
    size, width = out_ref.shape
    part = size // naux
    own, last = [], []
    for member in range(naux):
        row = jnp.concatenate([old_ref[member], jnp.zeros((share, width - nsq), F32)], axis=1)
        own.append(jnp.concatenate([row, jnp.zeros((part - share, width), F32)], axis=0))
        last.append(
            jnp.concatenate(
                [
                    old_ref[naux][:, member * slab : (member + 1) * slab],
                    jnp.zeros((share, 2 * LANES - slab), F32),
                ],
                axis=1,
            )
        )
    own, last = jnp.concatenate(own, axis=0), jnp.concatenate(last, axis=0).astype(BF)
    spread(share * naux, naux, own, last, None, out_ref)


def pack_kernel(route_ref, arrived_ref, old_ref, out_ref):
    size = out_ref.shape[0]
    handed = mm(route_ref[...], arrived_ref[...])
    tiles = handed.shape[0] // size
    for x in range(tiles):
        low = x * LANES
        piece = handed[x * size : (x + 1) * size] + old_ref[:, low : low + LANES].astype(F32)
        out_ref[:, low : low + LANES] = piece.astype(BF)
    out_ref[:, tiles * LANES :] = old_ref[:, tiles * LANES :]


def block_mask(rows, row_block, cols, col_block):
    row = lax.broadcasted_iota(jnp.int32, (rows, cols), 0) // row_block
    return row == lax.broadcasted_iota(jnp.int32, (rows, cols), 1) // col_block


def fetch_order(naux, chunk, wide=None):
    size = naux * 6 * chunk
    here = jnp.arange(size)
    k, source, piece = here // (naux * chunk), (here // chunk) % naux, here % chunk
    at = k * chunk + piece
    if wide is None:
        spot = source * 6 * chunk + at
    else:
        share, part, tiles = wide
        size = tiles * naux * part
        spot = (at % tiles) * (naux * part) + source * part + share + at // tiles
    return (spot[:, None] == jnp.arange(size)[None, :]).astype(BF)


def project(naux, chunk, ordered, covers, pieces):
    npno, width = covers.shape[1], covers.shape[0]
    half_rows = naux * chunk
    stack = []
    for k in range(3):
        block = ordered[k * half_rows : (k + 1) * half_rows]
        stack += [block[:, :npno], block[:, npno:]]
    stack = jnp.concatenate(stack, axis=0).astype(BF)
    mask = block_mask(3 * npno, npno, width, width // 3)
    half = jnp.where(mask, mm_nt(stack, covers), 0.0).astype(BF)
    return mm_tn(pieces, half).astype(BF)


def residual(naux, chunk, new, covers, pieces, matrix):
    npno, width = covers.shape[1], covers.shape[0]
    half_rows = naux * chunk
    mask = block_mask(3 * npno, npno, width, width // 3)
    high, low = high_low(mm_nt(new, matrix))
    left = jnp.where(mask, mm(pieces, high) + mm(pieces, low), 0.0)
    high, low = high_low(left)
    back = mm(high, covers) + mm(low, covers)
    packed = []
    for k in range(3):
        block = back[2 * k * half_rows : 2 * (k + 1) * half_rows]
        packed.append(jnp.concatenate([block[:half_rows], block[half_rows:]], axis=1))
    return jnp.concatenate(packed, axis=0)


def project_both(naux, chunk, order, came, cover_ref, piece_ref):
    ordered = mm(order, came)
    rows = ordered.shape[0] // 2
    return [
        project(
            naux, chunk, ordered[w * rows : (w + 1) * rows], cover_ref[w], piece_ref[w]
        )
        for w in range(2)
    ]


def work_both(naux, chunk, projs, cover_ref, piece_ref, col_ref, row_ref, states, mats):
    wide = mats[0].shape[1]
    start = up(wide, LANES)
    spans = ((0, wide), (start, start + mats[1].shape[1]))
    new, sent = [], []
    for w in range(2):
        den = col_ref[w] + row_ref[:, spans[w][0] : spans[w][1]]
        new.append((SHIFT_LEVEL * states[w] + mm(projs[w], mats[w])) / den)
    halves = [x.astype(BF) for x in new]
    for w in range(2):
        sent.append(residual(naux, chunk, halves[w], cover_ref[w], piece_ref[w], mats[w]))
    return new, halves, jnp.concatenate(sent, axis=0).astype(BF)


def relayout_kernel(ntno, share, rows_ref, own_ref, last_ref, wide_ref):
    nsq = ntno * ntno
    wide_ref[...] = rows_ref[...].astype(F32)
    own = [wide_ref[pl.ds(b, ntno, stride=ntno), :] for b in range(ntno)]
    last = [wide_ref[pl.ds(nsq + b * ntno, ntno), :] for b in range(share)]
    for parts, out in ((own, own_ref), (last, last_ref)):
        out[...] = jnp.concatenate(
            [
                jnp.concatenate([x[:, m * ntno : (m + 1) * ntno] for x in parts], axis=1)
                for m in range(3)
            ],
            axis=0,
        ).astype(BF)


def first_kernel(
    naux,
    chunk,
    came_ref,
    order_ref,
    later_order_ref,
    cover_ref,
    piece_ref,
    col_ref,
    row_ref,
    own_mat_ref,
    last_mat_ref,
    sent_ref,
    own_ref,
    last_ref,
):
    ntno, nsq = own_ref.shape
    slab = last_ref.shape[1]
    came = came_ref[...]
    pieces = gather_pieces(came)
    projs = project_both(naux, chunk, order_ref[...], pieces, cover_ref, piece_ref)
    old = mm(row_spots(ntno, naux, came.shape[0]), came)
    old_last = gather_last(ntno, naux, came)
    new, _, sent = work_both(
        naux,
        chunk,
        projs,
        cover_ref,
        piece_ref,
        col_ref,
        row_ref,
        (old[:, :nsq], old_last[:, :slab]),
        (own_mat_ref[...], last_mat_ref[...]),
    )
    own_ref[...] = new[0]
    last_ref[...] = new[1]
    sent_ref[...] = mm_tn(later_order_ref[...], sent).astype(BF)


def later_kernel(
    naux,
    chunk,
    came_ref,
    order_ref,
    cover_ref,
    piece_ref,
    col_ref,
    row_ref,
    own_ref,
    last_ref,
    own_mat_ref,
    last_mat_ref,
    sent_ref,
    new_ref,
):
    nsq, slab = own_ref.shape[1], last_ref.shape[1]
    start = up(nsq, LANES)
    projs = project_both(naux, chunk, order_ref[...], came_ref[...], cover_ref, piece_ref)
    _, halves, sent = work_both(
        naux,
        chunk,
        projs,
        cover_ref,
        piece_ref,
        col_ref,
        row_ref,
        (own_ref[...], last_ref[...]),
        (own_mat_ref[...], last_mat_ref[...]),
    )
    new_ref[...] = jnp.zeros(new_ref.shape, BF)
    new_ref[:, :nsq] = halves[0]
    new_ref[:, start : start + slab] = halves[1]
    sent_ref[...] = mm_tn(order_ref[...], sent).astype(BF)


def finish_kernel(came_ref, out_ref):
    nsq = out_ref.shape[2]
    naux = came_ref.shape[0]
    start, slab = up(nsq, LANES), nsq // naux
    last = []
    for member in range(naux):
        rows = came_ref[member].astype(F32)
        out_ref[member] = rows[:, :nsq]
        last.append(rows[:, start : start + slab])
    out_ref[naux] = jnp.concatenate(last, axis=1)


def body(
    aux_blocks,
    occ_blocks,
    intersections,
    tno_energy,
    occ_energy,
    tno_rank,
    triples_old,
    pair_amps,
    pno_energy,
    pair_occ,
    pair_rank,
    request_owner,
    request_row,
):
    tdev = aux_blocks.shape[0]
    ntno = tno_energy.shape[1]
    npno = pno_energy.shape[1]
    pdev = pair_amps.shape[0]
    naux = lax.axis_size("aux")
    ntrip = lax.axis_size("trip")
    member = lax.axis_index("aux")
    share = ntno // naux
    nreq = 3 * tdev
    nsq = ntno * ntno
    slab = share * ntno
    start = up(nsq, LANES)
    span = start + up(slab, LANES)
    prow = npno // naux
    chunk = prow * npno // LANES
    slots = ntrip * chunk
    owner = request_owner.reshape(nreq)

    blocks, asking = integral_blocks(
        aux_blocks, occ_blocks, request_owner, request_row, naux, ntrip, chunk
    )
    rows = lax.psum_scatter(blocks, "aux", scatter_dimension=0, tiled=True)[0]
    serve = swap(asking, "trip").reshape(slots, LANES)

    def routing(dest, at):
        k, part = at // chunk, at % chunk
        request = jnp.where(k < 3, 3 * dest + k, 3 * naux + k - 3)
        asked = jnp.sum(
            jnp.where(request[:, None] == jnp.arange(nreq)[None, :], owner[None, :], 0), axis=1
        )
        return ((asked * chunk + part)[:, None] == jnp.arange(slots)[None, :]).astype(BF)

    number = jnp.arange(naux * 6 * chunk)
    route = routing(number // (6 * chunk), number % (6 * chunk))
    part = 8
    tiles = 6 * chunk // (part - share)
    size, width = naux * part, start
    number = jnp.arange(tiles * size)
    place = number % part
    route_first = routing(
        (number % size) // part, jnp.maximum(place - share, 0) * tiles + number // size
    )
    route_first = jnp.where((place >= share)[:, None], route_first, jnp.zeros((), BF))
    packed_old = call(
        functools.partial(old_kernel, naux), jax.ShapeDtypeStruct((size, width), BF)
    )(triples_old)
    route_back = route.T
    order = fetch_order(naux, chunk)
    order_first = fetch_order(naux, chunk, (share, part, tiles))

    live = jnp.arange(npno)[None, :] < pair_rank[:, None]
    live_p = lax.dynamic_slice_in_dim(live, member * prow, prow, 1)
    energy_p = lax.dynamic_slice_in_dim(pno_energy, member * prow, prow, 1)
    pair_keep = (live_p[:, :, None] & live[:, None, :]).reshape(pdev * chunk, LANES)
    pair_den = (
        energy_p[:, :, None] + pno_energy[:, None, :] + pair_occ[:, None, None] + SHIFT_LEVEL
    ).reshape(pdev * chunk, LANES)
    amps = (
        lax.dynamic_slice_in_dim(pair_amps, member * prow * npno, prow * npno, 1)
        .reshape(pdev * chunk, LANES)
        .astype(F32)
    )
    gain = jnp.zeros_like(amps)

    def two(x):
        return jnp.stack([lax.dynamic_slice_in_dim(x, member, 1, 0)[0], x[naux]])

    masked = jnp.where(jnp.arange(ntno)[None, :] < tno_rank[:, None], tno_energy, jnp.inf)
    energy = two(masked)
    col = two(masked - jnp.sum(occ_energy, axis=1)[:, None] + SHIFT_LEVEL)[:, :, None]
    energy_b = lax.dynamic_slice_in_dim(energy[1], member * share, share, 0)
    row = jnp.concatenate(
        [
            (energy[0][:, None] + energy[0][None, :]).reshape(nsq),
            jnp.zeros((start - nsq,), F32),
            (energy_b[:, None] + energy[1][None, :]).reshape(slab),
            jnp.zeros((span - start - slab,), F32),
        ]
    )[None, :]
    cover = two(intersections)
    flat = cover.transpose(0, 1, 3, 2).reshape(2, 3 * ntno, npno)
    split = cover.reshape(2, 3, npno // 2, 2, ntno).transpose(0, 1, 3, 2, 4)
    split = split.reshape(2, 3 * npno, ntno)

    ready = (
        (serve, route, route_first, route_back, order, order_first)
        + (pair_keep, pair_den, amps, flat, split, col, row, packed_old)
    )
    serve, route, route_first, route_back, order, order_first, *ready = (
        lax.optimization_barrier(ready)
    )
    pair_keep, pair_den, amps, flat, split, col, row, packed_old = ready
    for step in range(PASSES):
        outgoing = jnp.where(pair_keep, amps.astype(BF), jnp.zeros((), BF))
        pad = serve.shape[1] - outgoing.shape[0]
        found = mm(serve, jnp.pad(outgoing, ((0, pad), (0, 0)))).astype(BF)
        arrived = swap(found.reshape(ntrip, chunk, LANES), "trip").reshape(slots, LANES)
        if step == 0:
            packed = call(pack_kernel, jax.ShapeDtypeStruct((size, width), BF))(
                route_first, arrived, packed_old
            )
            came = swap(packed.reshape(naux, part, width), "aux")
        else:
            handed = mm(route, arrived).astype(BF).reshape(naux, 6 * chunk, LANES)
            came = swap(handed, "aux")
        if step == 0:
            own_mat, last_mat = call(
                functools.partial(relayout_kernel, ntno, share),
                (
                    jax.ShapeDtypeStruct((3 * ntno, nsq), BF),
                    jax.ShapeDtypeStruct((3 * ntno, slab), BF),
                ),
                [pltpu.VMEM(rows.shape, F32)],
            )(rows)
            sent, own, last = call(
                functools.partial(first_kernel, naux, chunk),
                (
                    jax.ShapeDtypeStruct((naux * 6 * chunk, LANES), BF),
                    jax.ShapeDtypeStruct((ntno, nsq), F32),
                    jax.ShapeDtypeStruct((ntno, slab), F32),
                ),
            )(
                came.reshape(-1, width),
                order_first,
                order,
                flat,
                split,
                col,
                row,
                own_mat,
                last_mat,
            )
            came = swap(sent.reshape(naux, 6 * chunk, LANES), "aux")
            sent = mm(route_back, came.reshape(naux * 6 * chunk, LANES))
        else:
            sent, new = call(
                functools.partial(later_kernel, naux, chunk),
                (
                    jax.ShapeDtypeStruct((naux * 6 * chunk, LANES), BF),
                    jax.ShapeDtypeStruct((ntno, span), BF),
                ),
            )(
                came.reshape(-1, LANES),
                order,
                flat,
                split,
                col,
                row,
                own,
                last,
                own_mat,
                last_mat,
            )
            new = lax.all_gather(new, "aux", axis=0, tiled=False)
            new = lax.dynamic_slice_in_dim(new, member * share, share, 1)
            triples_new = call(finish_kernel, jax.ShapeDtypeStruct((tdev, share, nsq), F32))(new)
            came = swap(sent.reshape(naux, 6 * chunk, LANES), "aux")
            sent = mm(route_back, came.reshape(naux * 6 * chunk, LANES))
        sent = sent.astype(BF).reshape(ntrip, chunk, LANES)
        came = swap(sent, "trip").reshape(slots, LANES)
        total = mm_tn(serve, came)[: pdev * chunk]
        change = jnp.where(pair_keep, total / pair_den, 0.0)
        gain = gain + change
        amps = amps + change

    gains = jnp.broadcast_to(gain.astype(BF)[None], (naux, pdev * chunk, LANES))
    gains, triples_new = lax.optimization_barrier((swap(gains, "aux"), triples_new))
    gains = gains.reshape(naux, pdev, prow * npno).transpose(1, 0, 2)
    pairs_new = pair_amps.astype(F32) + gains.reshape(pdev, npno * npno).astype(F32)
    return triples_new, pairs_new


def solution(mesh):
    in_specs = (
        P("trip", "aux", None),
        P("trip", "aux", None),
        P("trip", None, None, None),
        P("trip", None),
        P("trip", None),
        P("trip"),
        P("trip", "aux", None),
        P("trip", None),
        P("trip", None),
        P("trip"),
        P("trip"),
        P("trip", None, None),
        P("trip", None),
    )
    out_specs = (P("trip", "aux", None), P("trip", None))
    return jax.shard_map(body, mesh=mesh, in_specs=in_specs, out_specs=out_specs, check_vma=False)
```

```python
import functools
import jax
import jax.numpy as jnp
from jax import lax
from jax.experimental import pallas as pl
from jax.experimental.pallas import tpu as pltpu
from jax.sharding import PartitionSpec as P

PASSES = 2
SHIFT_LEVEL = 1.0
BF = jnp.bfloat16
F32 = jnp.float32
LANES = 128
VMEM_LIMIT = 48 * 2**20
VMEM_ALL = 63 * 2**20


def mm(x, y):
    return jnp.dot(x, y, preferred_element_type=F32)


def mm_nt(x, y):
    return lax.dot_general(x, y, (((1,), (1,)), ((), ())), preferred_element_type=F32)


def mm_tn(x, y):
    return lax.dot_general(x, y, (((0,), (0,)), ((), ())), preferred_element_type=F32)


def swap(x, axis):
    return lax.all_to_all(x, axis, split_axis=0, concat_axis=0, tiled=True)


def up(n, m):
    return -(-n // m) * m


def call(kernel, outs, scratch=(), limit=VMEM_LIMIT, **specs):
    return pl.pallas_call(
        kernel,
        out_shape=outs,
        scratch_shapes=list(scratch),
        **specs,
        compiler_params=pltpu.CompilerParams(vmem_limit_bytes=limit),
    )


def blocks_kernel(
    naux,
    share,
    aux_ref,
    occ_far_ref,
    owner_far_ref,
    local_far_ref,
    out_ref,
    asking_out_ref,
    held_ref,
    made_ref,
    last_ref,
    occ_ref,
    owner_ref,
    local_ref,
    asking_ref,
    in_sems,
    out_sems,
    more_sems,
):
    nsq, depth = held_ref.shape[1:]
    width = occ_ref.shape[1]
    ntno = share * naux
    groups = [naux // 2, 0]
    ends = [naux + 1, naux // 2]
    arriving = []
    for n, (t, end) in enumerate(zip(groups, ends)):
        part = pl.ds(t, end - t)
        copy = pltpu.make_async_copy(aux_ref.at[part], held_ref.at[part], in_sems.at[n])
        copy.start()
        arriving.append(copy)
    pairs = ((owner_far_ref, owner_ref), (local_far_ref, local_ref), (occ_far_ref, occ_ref))
    first = [pltpu.make_async_copy(x, y, more_sems.at[n]) for n, (x, y) in enumerate(pairs)]
    for copy in first:
        copy.start()
    for copy in first:
        copy.wait()
    chunk = asking_ref.shape[1]
    asking_ref[...] = jnp.zeros(asking_ref.shape, BF)
    piece = lax.broadcasted_iota(jnp.int32, (chunk, LANES), 0)
    lane = lax.broadcasted_iota(jnp.int32, (chunk, LANES), 1)
    for m in range(local_ref.shape[0]):
        for t in range(local_ref.shape[1]):
            hot = (lane == local_ref[m, t] * chunk + piece).astype(F32).astype(BF)
            asking_ref[pl.ds(owner_ref[m, 0, t], 1)] = hot[None]
    asked = pltpu.make_async_copy(asking_ref, asking_out_ref, more_sems.at[3])
    asked.start()

    none = jnp.zeros((LANES - width, depth), BF)
    zero = jnp.zeros((LANES, depth), BF)
    rest = made_ref.shape[1] - nsq - share * ntno
    leaving = []
    for n, (low, end) in enumerate(zip(groups, ends)):
        arriving[n].wait()
        if end > naux:
            right = jnp.concatenate([occ_ref[naux], none], axis=0)
            last_ref[:nsq, :] = mm_nt(held_ref[naux], right)
        top = min(end, naux)
        for t in range(low, top, 2):
            left = jnp.concatenate([held_ref[t], held_ref[t + 1]], axis=1)
            upper = jnp.concatenate([occ_ref[t], none, zero], axis=0)
            lower = jnp.concatenate([zero, occ_ref[t + 1], none], axis=0)
            both = mm_nt(left, jnp.concatenate([upper, lower], axis=1)).astype(BF)
            made_ref[t, :nsq, :] = both[:, :LANES]
            made_ref[t + 1, :nsq, :] = both[:, LANES:]
            for member in (t, t + 1):
                parts = [
                    last_ref[pl.ds(member * share + b, ntno, stride=ntno), :]
                    for b in range(share)
                ]
                parts.append(jnp.zeros((rest, LANES), F32))
                made_ref[member, nsq:, :] = jnp.concatenate(parts, axis=0).astype(BF)
        part = pl.ds(low, top - low)
        copy = pltpu.make_async_copy(made_ref.at[part], out_ref.at[part], out_sems.at[n])
        copy.start()
        leaving.append(copy)
    for copy in leaving:
        copy.wait()
    asked.wait()


def integral_blocks(aux_blocks, occ_blocks, request_owner, request_row, naux, ntrip, chunk):
    tdev, depth, nsq = aux_blocks.shape
    ntno = occ_blocks.shape[2] // 3
    share = ntno // naux
    rows = up(nsq + share * ntno, 16)
    far = pl.BlockSpec(memory_space=pltpu.HBM)
    return call(
        functools.partial(blocks_kernel, naux, share),
        (
            jax.ShapeDtypeStruct((naux, rows, LANES), BF),
            jax.ShapeDtypeStruct((ntrip, chunk, LANES), BF),
        ),
        [
            pltpu.VMEM((tdev, nsq, depth), BF),
            pltpu.VMEM((naux, rows, LANES), BF),
            pltpu.VMEM((nsq + ntno, LANES), F32),
            pltpu.VMEM((tdev, occ_blocks.shape[2], depth), BF),
            pltpu.SMEM((3, 1, tdev), jnp.int32),
            pltpu.SMEM((3, tdev), jnp.int32),
            pltpu.VMEM((ntrip, chunk, LANES), BF),
            pltpu.SemaphoreType.DMA((2,)),
            pltpu.SemaphoreType.DMA((2,)),
            pltpu.SemaphoreType.DMA((4,)),
        ],
        VMEM_ALL,
        in_specs=[far] * 4,
        out_specs=(far, far),
    )(
        aux_blocks.transpose(0, 2, 1),
        occ_blocks.transpose(0, 2, 1),
        request_owner.transpose(1, 2, 0),
        request_row.T,
    )


def row_spots(ntno, naux, size, parity=None):
    share, part = ntno // naux, size // naux
    a = lax.broadcasted_iota(jnp.int32, (ntno, size), 0)
    there = lax.broadcasted_iota(jnp.int32, (ntno, size), 1)
    member, place = a // share, a % share
    if parity is None:
        hit = member * part + place == there
    else:
        hit = (member * part + share + place // 2 == there) & (place % 2 == parity)
    return hit.astype(F32).astype(BF)


def spread(ntno, naux, own, last, pieces, out_ref):
    size, width = out_ref.shape
    share, part = ntno // naux, size // naux
    tiles = 0 if pieces is None else pieces.shape[0] // size
    first = width - 5 * LANES
    for parity in range(2):
        add = mm_tn(row_spots(ntno, naux, size, parity), last)
        low = first + 2 * parity * LANES
        out_ref[:, low : low + 2 * LANES] = (own[:, low : low + 2 * LANES] + add).astype(BF)
    for x in range(tiles):
        low = x * LANES
        piece = pieces[x * size : (x + 1) * size]
        out_ref[:, low : low + LANES] = (own[:, low : low + LANES] + piece).astype(BF)
    if tiles == 0:
        out_ref[:, :first] = own[:, :first].astype(BF)
    out_ref[:, first + 4 * LANES :] = own[:, first + 4 * LANES :].astype(BF)


def gather_last(ntno, naux, came):
    size, width = came.shape
    first = width - 5 * LANES
    return sum(
        mm(
            row_spots(ntno, naux, size, parity),
            came[:, first + 2 * parity * LANES : first + 2 * (parity + 1) * LANES],
        )
        for parity in range(2)
    )


def gather_pieces(came):
    tiles = came.shape[1] // LANES - 5
    return jnp.concatenate([came[:, x * LANES : (x + 1) * LANES] for x in range(tiles)], axis=0)


def old_kernel(naux, old_ref, out_ref):
    share, nsq = old_ref.shape[1:]
    slab = nsq // naux
    size, width = out_ref.shape
    part = size // naux
    own, last = [], []
    for member in range(naux):
        row = jnp.concatenate([old_ref[member], jnp.zeros((share, width - nsq), F32)], axis=1)
        own.append(jnp.concatenate([row, jnp.zeros((part - share, width), F32)], axis=0))
        last.append(
            jnp.concatenate(
                [
                    old_ref[naux][:, member * slab : (member + 1) * slab],
                    jnp.zeros((share, 2 * LANES - slab), F32),
                ],
                axis=1,
            )
        )
    own, last = jnp.concatenate(own, axis=0), jnp.concatenate(last, axis=0).astype(BF)
    spread(share * naux, naux, own, last, None, out_ref)


def pack_kernel(route_ref, arrived_ref, old_ref, out_ref):
    size = out_ref.shape[0]
    handed = mm(route_ref[...], arrived_ref[...])
    tiles = handed.shape[0] // size
    for x in range(tiles):
        low = x * LANES
        piece = handed[x * size : (x + 1) * size] + old_ref[:, low : low + LANES].astype(F32)
        out_ref[:, low : low + LANES] = piece.astype(BF)
    out_ref[:, tiles * LANES :] = old_ref[:, tiles * LANES :]


def block_mask(rows, row_block, cols, col_block):
    row = lax.broadcasted_iota(jnp.int32, (rows, cols), 0) // row_block
    return row == lax.broadcasted_iota(jnp.int32, (rows, cols), 1) // col_block


def fetch_order(naux, chunk, wide=None):
    size = naux * 6 * chunk
    here = jnp.arange(size)
    k, source, piece = here // (naux * chunk), (here // chunk) % naux, here % chunk
    at = k * chunk + piece
    if wide is None:
        spot = source * 6 * chunk + at
    else:
        share, part, tiles = wide
        size = tiles * naux * part
        spot = (at % tiles) * (naux * part) + source * part + share + at // tiles
    return (spot[:, None] == jnp.arange(size)[None, :]).astype(BF)


def project(naux, chunk, ordered, covers, pieces):
    npno, width = covers.shape[1], covers.shape[0]
    half_rows = naux * chunk
    stack = []
    for k in range(3):
        block = ordered[k * half_rows : (k + 1) * half_rows]
        stack += [block[:, :npno], block[:, npno:]]
    stack = jnp.concatenate(stack, axis=0).astype(BF)
    mask = block_mask(3 * npno, npno, width, width // 3)
    half = jnp.where(mask, mm_nt(stack, covers), 0.0).astype(BF)
    return mm_tn(pieces, half).astype(BF)


def residual(naux, chunk, new, covers, pieces, matrix):
    npno, width = covers.shape[1], covers.shape[0]
    half_rows = naux * chunk
    mask = block_mask(3 * npno, npno, width, width // 3)
    left = mm(pieces, mm_nt(new, matrix).astype(BF))
    back = mm(jnp.where(mask, left, 0.0).astype(BF), covers)
    packed = []
    for k in range(3):
        block = back[2 * k * half_rows : 2 * (k + 1) * half_rows]
        packed.append(jnp.concatenate([block[:half_rows], block[half_rows:]], axis=1))
    return jnp.concatenate(packed, axis=0)


def project_both(naux, chunk, order, came, cover_ref, piece_ref):
    ordered = mm(order, came)
    rows = ordered.shape[0] // 2
    return [
        project(
            naux, chunk, ordered[w * rows : (w + 1) * rows], cover_ref[w], piece_ref[w]
        )
        for w in range(2)
    ]


def work_both(naux, chunk, projs, cover_ref, piece_ref, col_ref, row_ref, states, mats):
    wide = mats[0].shape[1]
    start = up(wide, LANES)
    spans = ((0, wide), (start, start + mats[1].shape[1]))
    new, sent = [], []
    for w in range(2):
        den = col_ref[w] + row_ref[:, spans[w][0] : spans[w][1]]
        new.append((SHIFT_LEVEL * states[w] + mm(projs[w], mats[w])) / den)
    halves = [x.astype(BF) for x in new]
    for w in range(2):
        sent.append(residual(naux, chunk, halves[w], cover_ref[w], piece_ref[w], mats[w]))
    return new, halves, jnp.concatenate(sent, axis=0).astype(BF)


def relayout_kernel(ntno, share, rows_ref, own_ref, last_ref, wide_ref):
    nsq = ntno * ntno
    wide_ref[...] = rows_ref[...].astype(F32)
    own = [wide_ref[pl.ds(b, ntno, stride=ntno), :] for b in range(ntno)]
    last = [wide_ref[pl.ds(nsq + b * ntno, ntno), :] for b in range(share)]
    for parts, out in ((own, own_ref), (last, last_ref)):
        out[...] = jnp.concatenate(
            [
                jnp.concatenate([x[:, m * ntno : (m + 1) * ntno] for x in parts], axis=1)
                for m in range(3)
            ],
            axis=0,
        ).astype(BF)


def first_kernel(
    naux,
    chunk,
    came_ref,
    order_ref,
    later_order_ref,
    cover_ref,
    piece_ref,
    col_ref,
    row_ref,
    own_mat_ref,
    last_mat_ref,
    sent_ref,
    own_ref,
    last_ref,
):
    ntno, nsq = own_ref.shape
    slab = last_ref.shape[1]
    came = came_ref[...]
    pieces = gather_pieces(came)
    projs = project_both(naux, chunk, order_ref[...], pieces, cover_ref, piece_ref)
    old = mm(row_spots(ntno, naux, came.shape[0]), came)
    old_last = gather_last(ntno, naux, came)
    new, _, sent = work_both(
        naux,
        chunk,
        projs,
        cover_ref,
        piece_ref,
        col_ref,
        row_ref,
        (old[:, :nsq], old_last[:, :slab]),
        (own_mat_ref[...], last_mat_ref[...]),
    )
    own_ref[...] = new[0]
    last_ref[...] = new[1]
    sent_ref[...] = mm_tn(later_order_ref[...], sent).astype(BF)


def later_kernel(
    naux,
    chunk,
    came_ref,
    order_ref,
    cover_ref,
    piece_ref,
    col_ref,
    row_ref,
    own_ref,
    last_ref,
    own_mat_ref,
    last_mat_ref,
    sent_ref,
    new_ref,
):
    nsq, slab = own_ref.shape[1], last_ref.shape[1]
    start = up(nsq, LANES)
    projs = project_both(naux, chunk, order_ref[...], came_ref[...], cover_ref, piece_ref)
    _, halves, sent = work_both(
        naux,
        chunk,
        projs,
        cover_ref,
        piece_ref,
        col_ref,
        row_ref,
        (own_ref[...], last_ref[...]),
        (own_mat_ref[...], last_mat_ref[...]),
    )
    new_ref[...] = jnp.zeros(new_ref.shape, BF)
    new_ref[:, :nsq] = halves[0]
    new_ref[:, start : start + slab] = halves[1]
    sent_ref[...] = mm_tn(order_ref[...], sent).astype(BF)


def finish_kernel(came_ref, out_ref):
    nsq = out_ref.shape[2]
    naux = came_ref.shape[0]
    start, slab = up(nsq, LANES), nsq // naux
    last = []
    for member in range(naux):
        rows = came_ref[member].astype(F32)
        out_ref[member] = rows[:, :nsq]
        last.append(rows[:, start : start + slab])
    out_ref[naux] = jnp.concatenate(last, axis=1)


def body(
    aux_blocks,
    occ_blocks,
    intersections,
    tno_energy,
    occ_energy,
    tno_rank,
    triples_old,
    pair_amps,
    pno_energy,
    pair_occ,
    pair_rank,
    request_owner,
    request_row,
):
    tdev = aux_blocks.shape[0]
    ntno = tno_energy.shape[1]
    npno = pno_energy.shape[1]
    pdev = pair_amps.shape[0]
    naux = lax.axis_size("aux")
    ntrip = lax.axis_size("trip")
    member = lax.axis_index("aux")
    share = ntno // naux
    nreq = 3 * tdev
    nsq = ntno * ntno
    slab = share * ntno
    start = up(nsq, LANES)
    span = start + up(slab, LANES)
    prow = npno // naux
    chunk = prow * npno // LANES
    slots = ntrip * chunk
    owner = request_owner.reshape(nreq)

    blocks, asking = integral_blocks(
        aux_blocks, occ_blocks, request_owner, request_row, naux, ntrip, chunk
    )
    rows = lax.psum_scatter(blocks, "aux", scatter_dimension=0, tiled=True)[0]
    serve = swap(asking, "trip").reshape(slots, LANES)

    def routing(dest, at):
        k, part = at // chunk, at % chunk
        request = jnp.where(k < 3, 3 * dest + k, 3 * naux + k - 3)
        asked = jnp.sum(
            jnp.where(request[:, None] == jnp.arange(nreq)[None, :], owner[None, :], 0), axis=1
        )
        return ((asked * chunk + part)[:, None] == jnp.arange(slots)[None, :]).astype(BF)

    number = jnp.arange(naux * 6 * chunk)
    route = routing(number // (6 * chunk), number % (6 * chunk))
    part = 8
    tiles = 6 * chunk // (part - share)
    size, width = naux * part, start
    number = jnp.arange(tiles * size)
    place = number % part
    route_first = routing(
        (number % size) // part, jnp.maximum(place - share, 0) * tiles + number // size
    )
    route_first = jnp.where((place >= share)[:, None], route_first, jnp.zeros((), BF))
    packed_old = call(
        functools.partial(old_kernel, naux), jax.ShapeDtypeStruct((size, width), BF)
    )(triples_old)
    route_back = route.T
    order = fetch_order(naux, chunk)
    order_first = fetch_order(naux, chunk, (share, part, tiles))

    live = jnp.arange(npno)[None, :] < pair_rank[:, None]
    live_p = lax.dynamic_slice_in_dim(live, member * prow, prow, 1)
    energy_p = lax.dynamic_slice_in_dim(pno_energy, member * prow, prow, 1)
    pair_keep = (live_p[:, :, None] & live[:, None, :]).reshape(pdev * chunk, LANES)
    pair_den = (
        energy_p[:, :, None] + pno_energy[:, None, :] + pair_occ[:, None, None] + SHIFT_LEVEL
    ).reshape(pdev * chunk, LANES)
    amps = (
        lax.dynamic_slice_in_dim(pair_amps, member * prow * npno, prow * npno, 1)
        .reshape(pdev * chunk, LANES)
        .astype(F32)
    )
    gain = jnp.zeros_like(amps)

    def two(x):
        return jnp.stack([lax.dynamic_slice_in_dim(x, member, 1, 0)[0], x[naux]])

    masked = jnp.where(jnp.arange(ntno)[None, :] < tno_rank[:, None], tno_energy, jnp.inf)
    energy = two(masked)
    col = two(masked - jnp.sum(occ_energy, axis=1)[:, None] + SHIFT_LEVEL)[:, :, None]
    energy_b = lax.dynamic_slice_in_dim(energy[1], member * share, share, 0)
    row = jnp.concatenate(
        [
            (energy[0][:, None] + energy[0][None, :]).reshape(nsq),
            jnp.zeros((start - nsq,), F32),
            (energy_b[:, None] + energy[1][None, :]).reshape(slab),
            jnp.zeros((span - start - slab,), F32),
        ]
    )[None, :]
    cover = two(intersections)
    flat = cover.transpose(0, 1, 3, 2).reshape(2, 3 * ntno, npno)
    split = cover.reshape(2, 3, npno // 2, 2, ntno).transpose(0, 1, 3, 2, 4)
    split = split.reshape(2, 3 * npno, ntno)

    ready = (
        (serve, route, route_first, route_back, order, order_first)
        + (pair_keep, pair_den, amps, flat, split, col, row, packed_old)
    )
    serve, route, route_first, route_back, order, order_first, *ready = (
        lax.optimization_barrier(ready)
    )
    pair_keep, pair_den, amps, flat, split, col, row, packed_old = ready
    for step in range(PASSES):
        outgoing = jnp.where(pair_keep, amps.astype(BF), jnp.zeros((), BF))
        pad = serve.shape[1] - outgoing.shape[0]
        found = mm(serve, jnp.pad(outgoing, ((0, pad), (0, 0)))).astype(BF)
        arrived = swap(found.reshape(ntrip, chunk, LANES), "trip").reshape(slots, LANES)
        if step == 0:
            packed = call(pack_kernel, jax.ShapeDtypeStruct((size, width), BF))(
                route_first, arrived, packed_old
            )
            came = swap(packed.reshape(naux, part, width), "aux")
        else:
            handed = mm(route, arrived).astype(BF).reshape(naux, 6 * chunk, LANES)
            came = swap(handed, "aux")
        if step == 0:
            own_mat, last_mat = call(
                functools.partial(relayout_kernel, ntno, share),
                (
                    jax.ShapeDtypeStruct((3 * ntno, nsq), BF),
                    jax.ShapeDtypeStruct((3 * ntno, slab), BF),
                ),
                [pltpu.VMEM(rows.shape, F32)],
            )(rows)
            sent, own, last = call(
                functools.partial(first_kernel, naux, chunk),
                (
                    jax.ShapeDtypeStruct((naux * 6 * chunk, LANES), BF),
                    jax.ShapeDtypeStruct((ntno, nsq), F32),
                    jax.ShapeDtypeStruct((ntno, slab), F32),
                ),
            )(
                came.reshape(-1, width),
                order_first,
                order,
                flat,
                split,
                col,
                row,
                own_mat,
                last_mat,
            )
            came = swap(sent.reshape(naux, 6 * chunk, LANES), "aux")
            sent = mm(route_back, came.reshape(naux * 6 * chunk, LANES))
        else:
            sent, new = call(
                functools.partial(later_kernel, naux, chunk),
                (
                    jax.ShapeDtypeStruct((naux * 6 * chunk, LANES), BF),
                    jax.ShapeDtypeStruct((ntno, span), BF),
                ),
            )(
                came.reshape(-1, LANES),
                order,
                flat,
                split,
                col,
                row,
                own,
                last,
                own_mat,
                last_mat,
            )
            new = lax.all_gather(new, "aux", axis=0, tiled=False)
            new = lax.dynamic_slice_in_dim(new, member * share, share, 1)
            triples_new = call(finish_kernel, jax.ShapeDtypeStruct((tdev, share, nsq), F32))(new)
            came = swap(sent.reshape(naux, 6 * chunk, LANES), "aux")
            sent = mm(route_back, came.reshape(naux * 6 * chunk, LANES))
        sent = sent.astype(BF).reshape(ntrip, chunk, LANES)
        came = swap(sent, "trip").reshape(slots, LANES)
        total = mm_tn(serve, came)[: pdev * chunk]
        change = jnp.where(pair_keep, total / pair_den, 0.0)
        gain = gain + change
        amps = amps + change

    gains = jnp.broadcast_to(gain.astype(BF)[None], (naux, pdev * chunk, LANES))
    gains, triples_new = lax.optimization_barrier((swap(gains, "aux"), triples_new))
    gains = gains.reshape(naux, pdev, prow * npno).transpose(1, 0, 2)
    pairs_new = pair_amps.astype(F32) + gains.reshape(pdev, npno * npno).astype(F32)
    return triples_new, pairs_new


def solution(mesh):
    in_specs = (
        P("trip", "aux", None),
        P("trip", "aux", None),
        P("trip", None, None, None),
        P("trip", None),
        P("trip", None),
        P("trip"),
        P("trip", "aux", None),
        P("trip", None),
        P("trip", None),
        P("trip"),
        P("trip"),
        P("trip", None, None),
        P("trip", None),
    )
    out_specs = (P("trip", "aux", None), P("trip", None))
    return jax.shard_map(body, mesh=mesh, in_specs=in_specs, out_specs=out_specs, check_vma=False)
```
